128 devices in a mesh: dp: 16 (over x_lo, z, core), expert: 8 (over x_hi, y).
Axes of the slice: x: 4 (x_hi: 2, x_lo: 2; x = x_hi * 2 + x_lo), y: 4, z: 4, core: 2. Of those that a mesh axis runs over, the one named last changes fastest.
Arguments:
- value_input: bfloat16 [16384, 4096], P(('dp', 'expert')), may hold values from -2.5 to 2.5
- value_grad: bfloat16 [16384, 512], P(('dp', 'expert')), may hold values from -0.625 to 0.625
- value_weight: bfloat16 [4096, 512], P('dp'), may hold values from -0.75 to 0.75
- out_grad: bfloat16 [16384, 4096], P(('dp', 'expert')), may hold values from -6 to 6
- route_ids: int32 [16384, 8], P(('dp', 'expert')), may hold values from 0 to 127, as said below
- route_slots: int32 [16384, 8], P(('dp', 'expert')), may hold values from 0 to 7, as said below
- seq_lengths: int32 [128], P(('dp', 'expert')), may hold values from 16 to 128, as said below
- route_weights: bfloat16 [16384, 8], P(('dp', 'expert')), may hold values from 0.019897461 to 0.5
- gate_act: bfloat16 [128, 128, 8, 768], P(('dp', 'expert')), may hold values from -8 to 8
- up_act: bfloat16 [128, 128, 8, 768], P(('dp', 'expert')), may hold values from -6 to 6
- w_gate: bfloat16 [128, 4096, 768], P(('dp', 'expert')), may hold values from -0.09375 to 0.09375
- w_up: bfloat16 [128, 4096, 768], P(('dp', 'expert')), may hold values from -0.09375 to 0.09375
- w_down: bfloat16 [128, 768, 4096], P(('dp', 'expert')), may hold values from -0.21875 to 0.21875
Outputs:
- moe_input_grad: bfloat16 [16384, 4096], P(('dp', 'expert'))
- weight_grad: bfloat16 [16384, 8], P(('dp', 'expert'))
- value_input_grad: bfloat16 [16384, 4096], P(('dp', 'expert'))
- value_weight_grad: float32 [4096, 512], P(('dp', 'expert'))
The draws below stay inside these ranges and needn't reach their ends.
Inputs may be any that keep to these rules, and one draw needn't show every extreme that they name: `route_ids`: each token names 8 different experts; the 128 tokens of one device name every expert exactly 8 times. `route_slots`: among the tokens of one device, the choices that name one expert hold the slots 0 to 7 once each, in order of token and then of choice. `seq_lengths`: some sequence has all 128 tokens live.
All inputs are finite; a program needn't handle non-finite values.
Results may differ from the reference program's by a relative error of at most 0.0057.
Values may be sent and summed in bfloat16 or wider, within the bound.
No kernel may reach another device: no remote copies, remote signals or barrier semaphores. Data moves between devices by JAX's collectives and lax.ppermute only.
A program may use at most 192 MiB of HBM per device.

```python
import math
import jax
import jax.numpy as jnp
from jax import lax

D = 4096
FFW = 768
KVW = 512
TOPK = 8
TOK_DEV = 128
EXPERTS = 128
TOKENS = 16384
CAP = 8
N_DP = 16
N_EXPERT = 8


def routing(key):
    blocks = TOKENS // TOK_DEV
    block_keys = jax.random.split(key, blocks)
    stride = EXPERTS // TOPK

    def draw_block(block_key):
        order_key, label_key = jax.random.split(block_key)
        token_order = jax.random.permutation(order_key, TOK_DEV).astype(jnp.int32)
        relabel = jax.random.permutation(label_key, EXPERTS).astype(jnp.int32)
        base_expert = token_order % EXPERTS
        raw_ids = (base_expert[:, None] + stride * jnp.arange(TOPK, dtype=jnp.int32)[None, :]) % EXPERTS
        expert_ids = relabel[raw_ids].astype(jnp.int32)
        flat_ids = expert_ids.reshape(-1)
        positions = jnp.arange(TOK_DEV * TOPK, dtype=jnp.int32)
        earlier = positions[:, None] > positions[None, :]
        same = flat_ids[:, None] == flat_ids[None, :]
        slot_ids = jnp.sum((same & earlier).astype(jnp.int32), axis=1).reshape(TOK_DEV, TOPK)
        return (expert_ids, slot_ids.astype(jnp.int32))
    expert_ids, slot_ids = lax.map(draw_block, block_keys)
    return (expert_ids.reshape(TOKENS, TOPK), slot_ids.reshape(TOKENS, TOPK))


def draw_route_ids(key, part):
    shared = routing(key)
    return shared[0]


def draw_route_slots(key, part):
    shared = routing(key)
    return shared[1]


def draw_seq_lengths(key, part):
    key = jax.random.fold_in(key, 23)
    length_key, full_key = jax.random.split(key)
    sequences = TOKENS // TOK_DEV
    lengths = jax.random.randint(length_key, (sequences,), TOK_DEV // 8, TOK_DEV + 1, dtype=jnp.int32)
    full_index = jax.random.randint(full_key, (), 0, sequences, dtype=jnp.int32)
    return lengths.at[full_index].set(TOK_DEV).astype(jnp.int32)


def strengthened(result, rng, source, target, parts, factor):
    def block_of(position):
        return (jnp.arange(result.shape[position]) // (result.shape[position] // parts)).reshape((-1,) + (1,) * (result.ndim - 1 - position))

    near = jax.random.permutation(rng, parts)[block_of(target)]
    other_side = (block_of(target) + parts // 2) % parts
    return jnp.where((block_of(source) == near) | (block_of(source) == other_side), factor * result, result)


def levels(key, shape, shards, smallest, high):
    def one(axis_at, shards_of):
        steps = jax.random.uniform(jax.random.fold_in(jax.random.fold_in(key, 6), axis_at), (shards_of,), jnp.float32, smallest / len(shards), high / len(shards))
        return jnp.repeat(jnp.exp(steps), shape[axis_at] // shards_of).reshape((-1,) + (1,) * (len(shape) - axis_at - 1))

    gain = one(*shards[0])
    for cut in shards[1:]:
        gain = gain * one(*cut)
    return gain


def noise(own_key, extent, spread, reach, pieces=(), kind=jnp.bfloat16):
    loudness = levels(own_key, extent, pieces, -0.22, 0.18) if pieces else 1.0
    array = jax.random.normal(own_key, extent, jnp.float32) * spread * loudness
    return jnp.minimum(jnp.maximum(array, -reach), reach).astype(kind)


def gaussian_with(own_key, dims, scale, reach, cuts, heavy, kind=jnp.bfloat16):
    entries = scale * jax.random.normal(own_key, dims, jnp.float32)
    if cuts:
        entries = entries * levels(own_key, dims, cuts, -0.22, 0.18)
    return jnp.clip(strengthened(entries, jax.random.fold_in(own_key, 3), *heavy), -reach, reach).astype(kind)


def setup_inputs(seed: int = 0) -> dict:
    seeds = jax.random.split(jax.random.key(seed), 14)
    return {
        "value_input": gaussian_with(seeds[0], (TOKENS, D), 0.1, 2.5, ((0, 128),), (0, 1, 128, 5.5)),
        "value_grad": noise(seeds[1], (TOKENS, KVW), 0.1, 0.625, ((0, 128),)),
        "value_weight": noise(seeds[2], (D, KVW), (KVW // 8) ** -0.5, 0.75, ((0, 16),)),
        "out_grad": noise(seeds[3], (TOKENS, D), 1.0, 6.0, ((0, 128),)),
        "route_ids": draw_route_ids(jax.random.fold_in(seeds[13], 71), 0),
        "route_slots": draw_route_slots(jax.random.fold_in(seeds[13], 71), 0),
        "seq_lengths": draw_seq_lengths(jax.random.fold_in(seeds[13], 71), 0),
        "route_weights": jnp.clip(jnp.exp(math.log(0.5) - 3.224016 * jax.random.uniform(seeds[7], (TOKENS, TOPK), jnp.float32) ** levels(seeds[7], (TOKENS, TOPK), ((0, 128),), -0.2, 0.2)), 0.019897461, 0.5).astype(jnp.bfloat16),
        "gate_act": noise(seeds[8], (EXPERTS, N_DP * N_EXPERT, CAP, FFW), 1.5, 8.0, ((0, 128),)),
        "up_act": noise(seeds[9], (EXPERTS, N_DP * N_EXPERT, CAP, FFW), 1.0, 6.0, ((0, 128),)),
        "w_gate": noise(seeds[10], (EXPERTS, D, FFW), D ** -0.5, 0.09375, ((0, 128),)),
        "w_up": noise(seeds[11], (EXPERTS, D, FFW), D ** -0.5, 0.09375, ((0, 128),)),
        "w_down": noise(seeds[12], (EXPERTS, FFW, D), FFW ** -0.5, 0.21875, ((0, 128),)),
    }


def expert_grads(routed_rows, routed_weights, gate_saved, up_saved, gate_proj, up_proj, down_proj):
    back_proj = jnp.dot(routed_rows, down_proj.T, preferred_element_type=jnp.float32)
    gate_pre = gate_saved.astype(jnp.float32)
    up_pre = up_saved.astype(jnp.float32)
    gate_sigmoid = jax.nn.sigmoid(gate_pre)
    gate_silu = gate_pre * gate_sigmoid
    weight_grads = jnp.sum(back_proj * gate_silu * up_pre, axis=1).astype(jnp.bfloat16)
    scaled = routed_weights.astype(jnp.float32)[:, None] * back_proj
    up_grad = (scaled * gate_silu).astype(jnp.bfloat16)
    gate_grad = (scaled * up_pre * gate_sigmoid * (1.0 + gate_pre * (1.0 - gate_sigmoid))).astype(jnp.bfloat16)
    input_grads = jnp.dot(gate_grad, gate_proj.T, preferred_element_type=jnp.float32)
    input_grads = input_grads + jnp.dot(up_grad, up_proj.T, preferred_element_type=jnp.float32)
    return input_grads.astype(jnp.bfloat16), weight_grads


def reference(value_input, value_grad, value_weight, out_grad, route_ids, route_slots, seq_lengths, route_weights, gate_act, up_act, w_gate, w_up, w_down):
    source_total = N_DP * N_EXPERT
    token_index = jnp.arange(TOKENS, dtype=jnp.int32)
    source_dev = token_index // TOK_DEV
    live_mask = (token_index % TOK_DEV) < seq_lengths[source_dev]
    target = jnp.where(live_mask[:, None], route_ids, EXPERTS).astype(jnp.int32)
    column = (source_dev[:, None] * CAP + route_slots).astype(jnp.int32)
    row_buffer = jnp.zeros((EXPERTS, source_total * CAP, D), jnp.bfloat16)
    weight_buffer = jnp.zeros((EXPERTS, source_total * CAP), jnp.bfloat16)
    for rank in range(TOPK):
        row_buffer = row_buffer.at[target[:, rank], column[:, rank]].set(out_grad, mode="drop")
        weight_buffer = weight_buffer.at[target[:, rank], column[:, rank]].set(route_weights[:, rank], mode="drop")
    gate_rows = gate_act.reshape(EXPERTS, source_total * CAP, FFW)
    up_rows = up_act.reshape(EXPERTS, source_total * CAP, FFW)

    def per_expert(operands):
        return expert_grads(*operands)

    input_grads, weight_grads = lax.map(per_expert, (row_buffer, weight_buffer, gate_rows, up_rows, w_gate, w_up, w_down))
    safe_ids = jnp.where(live_mask[:, None], route_ids, 0).astype(jnp.int32)
    moe_sum = jnp.zeros((TOKENS, D), jnp.float32)
    weight_cols = []
    for rank in range(TOPK):
        picked = input_grads[safe_ids[:, rank], column[:, rank]]
        moe_sum = moe_sum + jnp.where(live_mask[:, None], picked.astype(jnp.float32), jnp.zeros((), jnp.float32))
        chosen = weight_grads[safe_ids[:, rank], column[:, rank]]
        weight_cols.append(jnp.where(live_mask, chosen, jnp.zeros((), chosen.dtype)))
    weight_grad = jnp.stack(weight_cols, axis=1)
    value_input_grad = jnp.dot(value_grad, value_weight.T, preferred_element_type=jnp.float32).astype(jnp.bfloat16)
    value_weight_grad = jnp.dot(value_input.T, value_grad, preferred_element_type=jnp.float32)
    return (moe_sum.astype(jnp.bfloat16), weight_grad, value_input_grad, value_weight_grad)
```

```python
import functools

import jax
import jax.numpy as jnp
from jax import lax
from jax.experimental import pallas as pl
from jax.experimental.pallas import tpu as pltpu
from jax.sharding import PartitionSpec as P

AXES = ("dp", "expert")
MIB = 1024 * 1024
NT = (((1,), (1,)), ((), ()))


def dot_nt(left, right):
    return lax.dot_general(left, right, NT, preferred_element_type=jnp.float32)


def exchange(array, axes):
    return lax.all_to_all(array, axes, split_axis=0, concat_axis=0, tiled=True)


def rows_kernel(slot_ref, grad_ref, out_ref):
    rows, width = out_ref.shape
    tokens = grad_ref.shape[0]
    slot = lax.broadcasted_iota(jnp.int32, (rows, tokens), 0) + pl.program_id(0) * rows
    hit = slot_ref[0:1, :] == slot
    for k in range(1, slot_ref.shape[0]):
        hit = hit | (slot_ref[k : k + 1, :] == slot)
    pick = jnp.where(hit, 1.0, 0.0).astype(jnp.bfloat16)
    step = min(width, 1024)
    for c in range(0, width, step):
        out_ref[:, c : c + step] = jnp.dot(
            pick, grad_ref[:, c : c + step], preferred_element_type=jnp.float32
        ).astype(jnp.bfloat16)


def build_rows(slot_t, out_grad, start, width, slots):
    tokens = out_grad.shape[0]
    rows = 256
    return pl.pallas_call(
        rows_kernel,
        grid=(slots // rows,),
        in_specs=[
            pl.BlockSpec(slot_t.shape, lambda i: (0, 0)),
            pl.BlockSpec((tokens, width), lambda i: (0, start // width)),
        ],
        out_specs=pl.BlockSpec((rows, width), lambda i: (i, 0)),
        out_shape=jax.ShapeDtypeStruct((slots, width), jnp.bfloat16),
        compiler_params=pltpu.CompilerParams(vmem_limit_bytes=32 * MIB),
        cost_estimate=pl.CostEstimate(
            flops=2 * slots * tokens * width, bytes_accessed=2 * (slots + tokens) * width, transcendentals=0
        ),
        name="build_rows",
    )(slot_t, out_grad)


def hidden_kernel(x_ref, down_ref, gate_ref, up_ref, hidden_ref, score_ref, acc_ref):
    k = pl.program_id(0)
    rows, ffw = acc_ref.shape
    part = 256

    @pl.when(k == 0)
    def _():
        acc_ref[...] = jnp.zeros_like(acc_ref)

    for r in range(0, rows, part):
        acc_ref[r : r + part, :] += dot_nt(x_ref[r : r + part, :], down_ref[...])

    @pl.when(k == pl.num_programs(0) - 1)
    def _():
        for r in range(0, rows, part):
            here = slice(r, r + part)
            back = acc_ref[here, :]
            gate = gate_ref[here, :].astype(jnp.float32)
            up = up_ref[here, :].astype(jnp.float32)
            sig = 1.0 / (1.0 + jnp.exp(-gate))
            silu = gate * sig
            up_grad = back * silu
            hidden_ref[here, ffw:] = up_grad.astype(jnp.bfloat16)
            hidden_ref[here, :ffw] = (back * up * sig * (1.0 + gate * (1.0 - sig))).astype(jnp.bfloat16)
            term = up_grad * up
            lanes = term[:, 0:128]
            for c in range(128, ffw, 128):
                lanes = lanes + term[:, c : c + 128]
            score_ref[:, here] = jnp.sum(lanes.T, axis=0, keepdims=True)


def hidden_grads(rows_in, down, gate, up):
    slots, width = rows_in.shape
    ffw = down.shape[0]
    block = 512
    return pl.pallas_call(
        hidden_kernel,
        grid=(width // block,),
        in_specs=[
            pl.BlockSpec((slots, block), lambda k: (0, k)),
            pl.BlockSpec((ffw, block), lambda k: (0, k)),
            pl.BlockSpec((slots, ffw), lambda k: (0, 0)),
            pl.BlockSpec((slots, ffw), lambda k: (0, 0)),
        ],
        out_specs=[
            pl.BlockSpec((slots, 2 * ffw), lambda k: (0, 0)),
            pl.BlockSpec((1, slots), lambda k: (0, 0)),
        ],
        out_shape=[
            jax.ShapeDtypeStruct((slots, 2 * ffw), jnp.bfloat16),
            jax.ShapeDtypeStruct((1, slots), jnp.float32),
        ],
        scratch_shapes=[pltpu.VMEM((slots, ffw), jnp.float32)],
        compiler_params=pltpu.CompilerParams(vmem_limit_bytes=48 * MIB),
        cost_estimate=pl.CostEstimate(
            flops=2 * slots * width * ffw,
            bytes_accessed=2 * (slots * width + ffw * width + 4 * slots * ffw),
            transcendentals=slots * ffw,
        ),
        name="hidden_grads",
    )(rows_in, down, gate, up)


def slot_kernel(hidden_ref, gate_w_ref, up_w_ref, out_ref):
    ffw = gate_w_ref.shape[1]
    rows = out_ref.shape[0]
    part = 256
    for r in range(0, rows, part):
        here = slice(r, r + part)
        out_ref[here, :] = (
            dot_nt(hidden_ref[here, :ffw], gate_w_ref[...]) + dot_nt(hidden_ref[here, ffw:], up_w_ref[...])
        ).astype(jnp.bfloat16)


def slot_grads(hidden, gate_w, up_w, start, width):
    slots = hidden.shape[0]
    ffw = gate_w.shape[1]
    block = 512
    first = start // block
    return pl.pallas_call(
        slot_kernel,
        grid=(width // block,),
        in_specs=[
            pl.BlockSpec((slots, 2 * ffw), lambda j: (0, 0)),
            pl.BlockSpec((block, ffw), lambda j: (first + j, 0)),
            pl.BlockSpec((block, ffw), lambda j: (first + j, 0)),
        ],
        out_specs=pl.BlockSpec((slots, block), lambda j: (0, j)),
        out_shape=jax.ShapeDtypeStruct((slots, width), jnp.bfloat16),
        compiler_params=pltpu.CompilerParams(vmem_limit_bytes=48 * MIB),
        cost_estimate=pl.CostEstimate(
            flops=4 * slots * width * ffw,
            bytes_accessed=2 * (slots * width + 2 * ffw * width + 2 * slots * ffw),
            transcendentals=0,
        ),
        name="slot_grads",
    )(hidden, gate_w, up_w)


def combine_kernel(slot_ref, weight_ref, rows_ref, out_ref, mix_ref):
    @pl.when(pl.program_id(0) == 0)
    def _():
        slot = lax.broadcasted_iota(jnp.int32, mix_ref.shape, 1)
        mix = jnp.zeros(mix_ref.shape, jnp.float32)
        for k in range(slot_ref.shape[1]):
            mix = mix + jnp.where(slot_ref[:, k : k + 1] == slot, weight_ref[:, k : k + 1], 0.0)
        mix_ref[...] = mix.astype(jnp.bfloat16)

    out_ref[...] = jnp.dot(mix_ref[...], rows_ref[...], preferred_element_type=jnp.float32).astype(jnp.bfloat16)


def combine(slot, weight, returned):
    slots, width = returned.shape
    tokens = slot.shape[0]
    block = 512
    return pl.pallas_call(
        combine_kernel,
        grid=(width // block,),
        in_specs=[
            pl.BlockSpec(slot.shape, lambda j: (0, 0)),
            pl.BlockSpec(weight.shape, lambda j: (0, 0)),
            pl.BlockSpec((slots, block), lambda j: (0, j)),
        ],
        out_specs=pl.BlockSpec((tokens, block), lambda j: (0, j)),
        out_shape=jax.ShapeDtypeStruct((tokens, width), jnp.bfloat16),
        scratch_shapes=[pltpu.VMEM((tokens, slots), jnp.bfloat16)],
        compiler_params=pltpu.CompilerParams(vmem_limit_bytes=32 * MIB),
        cost_estimate=pl.CostEstimate(
            flops=2 * slots * tokens * width, bytes_accessed=2 * (slots + tokens) * width, transcendentals=0
        ),
        name="combine",
    )(slot, weight, returned)


def body(
    value_input,
    value_grad,
    value_weight,
    out_grad,
    route_ids,
    route_slots,
    seq_lengths,
    route_weights,
    gate_act,
    up_act,
    w_gate,
    w_up,
    w_down,
):
    tokens, width = out_grad.shape
    dp = lax.axis_size("dp")
    experts = lax.axis_size("expert")
    devices = dp * experts
    capacity = gate_act.shape[2]
    ffw = gate_act.shape[3]
    slots = devices * capacity

    live = jnp.arange(tokens, dtype=jnp.int32) < seq_lengths[0]
    slot = jnp.where(live[:, None], route_ids * capacity + route_slots, -1)

    with jax.named_scope("dispatch"):
        send = build_rows(slot.T, out_grad, 0, width, slots)
        routed = exchange(send.reshape(devices, capacity, width), AXES).reshape(slots, width)

    with jax.named_scope("value"):
        cols = width // dp
        grad_all = lax.all_gather(value_grad, "dp", axis=0, tiled=True)
        input_cols = value_input.reshape(tokens, dp, cols).transpose(1, 0, 2)
        input_all = exchange(input_cols, "dp").reshape(dp * tokens, cols)
        value_cols = jnp.einsum("tk,rk->tr", grad_all, value_weight, preferred_element_type=jnp.float32)
        value_cols = exchange(value_cols.astype(jnp.bfloat16).reshape(dp, tokens, cols), "dp")
        value_input_grad = value_cols.transpose(1, 0, 2).reshape(tokens, width)
        term = jnp.einsum("tr,tk->rk", input_all, grad_all, preferred_element_type=jnp.float32)
        terms = exchange(term.reshape(experts, cols // experts, term.shape[1]), "expert")
        value_weight_grad = jnp.sum(terms, axis=0)

    with jax.named_scope("experts"):
        hidden, score = hidden_grads(
            routed, w_down[0], gate_act.reshape(slots, ffw), up_act.reshape(slots, ffw)
        )
        slot_input = slot_grads(hidden, w_gate[0], w_up[0], 0, width)

    with jax.named_scope("return"):
        returned = exchange(slot_input.reshape(devices, capacity, width), AXES).reshape(slots, width)
        scores = exchange(score.astype(jnp.bfloat16).reshape(devices, 1, capacity), AXES).reshape(slots)
        moe_input_grad = combine(slot, route_weights.astype(jnp.float32), returned)
        weight_grad = jnp.sum(
            jnp.where(
                slot[:, :, None] == jnp.arange(slots, dtype=jnp.int32),
                scores.astype(jnp.float32),
                0.0,
            ),
            axis=2,
        ).astype(jnp.bfloat16)
    return (moe_input_grad, weight_grad, value_input_grad, value_weight_grad)


def solution(mesh):
    split = P(AXES, None)
    return jax.shard_map(
        body,
        mesh=mesh,
        in_specs=(
            split,
            split,
            P("dp", None),
            split,
            split,
            split,
            P(AXES),
            split,
            P(AXES, None, None, None),
            P(AXES, None, None, None),
            P(AXES, None, None),
            P(AXES, None, None),
            P(AXES, None, None),
        ),
        out_specs=(split, split, split, split),
        check_vma=False,
    )
```

```python
import functools

import jax
import jax.numpy as jnp
from jax import lax
from jax.experimental import pallas as pl
from jax.experimental.pallas import tpu as pltpu
from jax.sharding import PartitionSpec as P

AXES = ("dp", "expert")
MIB = 1024 * 1024
LANES = 128
CAPACITY = 8
NT = (((1,), (1,)), ((), ()))


def dot_nt(left, right):
    return lax.dot_general(left, right, NT, preferred_element_type=jnp.float32)


def exchange(array, axes):
    return lax.all_to_all(array, axes, split_axis=0, concat_axis=0, tiled=True)


def rows_kernel(length_ref, ids_ref, slots_ref, grad_ref, out_ref):
    rows, width = out_ref.shape
    top, tokens = ids_ref.shape
    live = lax.broadcasted_iota(jnp.int32, (1, tokens), 1) < length_ref[0]
    slot = lax.broadcasted_iota(jnp.int32, (rows, tokens), 0) + pl.program_id(0) * rows
    hit = None
    for k in range(top):
        name = jnp.where(live, ids_ref[k : k + 1, :] * CAPACITY + slots_ref[k : k + 1, :], -1)
        hit = name == slot if hit is None else hit | (name == slot)
    pick = jnp.where(hit, 1.0, 0.0).astype(jnp.bfloat16)
    step = 1024
    for c in range(0, width, step):
        out_ref[:, c : c + step] = jnp.dot(
            pick, grad_ref[:, c : c + step], preferred_element_type=jnp.float32
        ).astype(jnp.bfloat16)


def build_rows(seq_lengths, ids_t, slots_t, out_grad, slots):
    tokens, width = out_grad.shape
    rows = 256
    return pl.pallas_call(
        rows_kernel,
        grid=(slots // rows,),
        in_specs=[
            pl.BlockSpec(memory_space=pltpu.SMEM),
            pl.BlockSpec(ids_t.shape, lambda i: (0, 0)),
            pl.BlockSpec(slots_t.shape, lambda i: (0, 0)),
            pl.BlockSpec((tokens, width), lambda i: (0, 0)),
        ],
        out_specs=pl.BlockSpec((rows, width), lambda i: (i, 0)),
        out_shape=pltpu.HBM((slots, width), jnp.bfloat16),
        compiler_params=pltpu.CompilerParams(vmem_limit_bytes=32 * MIB),
        cost_estimate=pl.CostEstimate(
            flops=2 * slots * tokens * width, bytes_accessed=2 * (slots + tokens) * width, transcendentals=0
        ),
        name="build_rows",
    )(seq_lengths, *[pltpu.with_memory_space_constraint(a, pltpu.HBM) for a in (ids_t, slots_t, out_grad)])


def hidden_kernel(x_ref, down_ref, gate_ref, up_ref, hidden_ref, score_ref):
    rows = x_ref.shape[0]
    ffw = down_ref.shape[0]
    part = 256
    score = jnp.zeros((rows, LANES), jnp.float32)
    for c in range(0, ffw, part):
        cols = slice(c, c + part)
        back = dot_nt(x_ref[...], down_ref[cols, :])
        gate = gate_ref[:, cols].astype(jnp.float32)
        up = up_ref[:, cols].astype(jnp.float32)
        sig = 1.0 / (1.0 + jnp.exp(-gate))
        up_grad = back * (gate * sig)
        hidden_ref[:, ffw + c : ffw + c + part] = up_grad.astype(jnp.bfloat16)
        hidden_ref[:, cols] = (back * up * sig * (1.0 + gate * (1.0 - sig))).astype(jnp.bfloat16)
        term = up_grad * up
        for lane in range(0, part, LANES):
            score = score + term[:, lane : lane + LANES]
    score = jnp.sum(score, axis=1, keepdims=True)
    score_ref[...] = jnp.broadcast_to(score, score_ref.shape).astype(jnp.bfloat16)


def hidden_grads(rows_in, down, gate, up, score_at):
    slots, width = rows_in.shape
    ffw = down.shape[0]
    rows = 256
    return pl.pallas_call(
        hidden_kernel,
        grid=(slots // rows,),
        in_specs=[
            pl.BlockSpec((rows, width), lambda i: (i, 0)),
            pl.BlockSpec(memory_space=pltpu.VMEM),
            pl.BlockSpec((rows, ffw), lambda i: (i, 0)),
            pl.BlockSpec((rows, ffw), lambda i: (i, 0)),
        ],
        out_specs=[
            pl.BlockSpec((rows, 2 * ffw), lambda i: (i, 0)),
            pl.BlockSpec((rows, LANES), lambda i: (i, score_at // LANES)),
        ],
        out_shape=[
            jax.ShapeDtypeStruct((slots, 2 * ffw), jnp.bfloat16),
            pltpu.HBM((slots, score_at + LANES), jnp.bfloat16),
        ],
        compiler_params=pltpu.CompilerParams(vmem_limit_bytes=32 * MIB),
        cost_estimate=pl.CostEstimate(flops=1, bytes_accessed=1, transcendentals=0),
        name="hidden_grads",
    )(
        rows_in,
        pltpu.with_memory_space_constraint(down, pltpu.VMEM),
        pltpu.with_memory_space_constraint(gate, pltpu.HBM),
        pltpu.with_memory_space_constraint(up, pltpu.HBM),
    )


def slot_kernel(hidden_ref, gate_w_ref, up_w_ref, *refs):
    out_ref = refs[-1]
    ffw = gate_w_ref.shape[1]
    part = 256
    for r in range(0, out_ref.shape[0], part):
        here = slice(r, r + part)
        out_ref[here, :] = (
            dot_nt(hidden_ref[here, :ffw], gate_w_ref[...]) + dot_nt(hidden_ref[here, ffw:], up_w_ref[...])
        ).astype(jnp.bfloat16)


def slot_grads(hidden, gate_w, up_w, start, width, into=None):
    slots = hidden.shape[0]
    ffw = gate_w.shape[1]
    block = 512
    first = start // block
    before = () if into is None else (into,)
    cost = pl.CostEstimate(flops=1, bytes_accessed=1, transcendentals=0)
    if into is None:
        cost = pl.CostEstimate(
            flops=4 * slots * width * ffw,
            bytes_accessed=2 * (slots * width + 2 * ffw * width + 2 * slots * ffw),
            transcendentals=0,
        )
    return pl.pallas_call(
        slot_kernel,
        grid=(width // block,),
        in_specs=[
            pl.BlockSpec((slots, 2 * ffw), lambda j: (0, 0)),
            pl.BlockSpec((block, ffw), lambda j: (first + j, 0)),
            pl.BlockSpec((block, ffw), lambda j: (first + j, 0)),
        ]
        + [pl.BlockSpec(memory_space=pl.ANY)] * len(before),
        out_specs=pl.BlockSpec((slots, block), lambda j: (0, j)),
        out_shape=pltpu.HBM((slots, width if into is None else into.shape[1]), jnp.bfloat16),
        input_output_aliases={3: 0} if before else {},
        compiler_params=pltpu.CompilerParams(vmem_limit_bytes=32 * MIB),
        cost_estimate=cost,
        name="slot_grads",
    )(
        hidden,
        pltpu.with_memory_space_constraint(gate_w, pltpu.HBM),
        pltpu.with_memory_space_constraint(up_w, pltpu.HBM),
        *before,
    )


def mix_kernel(slot_ref, weight_ref, mix_ref):
    slot = lax.broadcasted_iota(jnp.int32, mix_ref.shape, 1)
    mix = jnp.zeros(mix_ref.shape, jnp.float32)
    for k in range(slot_ref.shape[1]):
        mix = mix + jnp.where(slot_ref[:, k : k + 1] == slot, weight_ref[:, k : k + 1], 0.0)
    mix_ref[...] = mix.astype(jnp.bfloat16)


def mix_weights(slot, weight, slots):
    return pl.pallas_call(
        mix_kernel,
        out_shape=jax.ShapeDtypeStruct((slot.shape[0], slots), jnp.bfloat16),
        name="mix_weights",
    )(slot, weight)


def combine_kernel(mix_ref, rows_ref, *refs):
    refs[-1][...] = jnp.dot(mix_ref[...], rows_ref[...], preferred_element_type=jnp.float32).astype(jnp.bfloat16)


def combine(mix, returned, start, cols, width, earlier=None):
    slots = returned.shape[0]
    tokens = mix.shape[0]
    block = 1024
    first = start // block
    before = () if earlier is None else (earlier,)
    return pl.pallas_call(
        combine_kernel,
        grid=(cols // block,),
        in_specs=[
            pl.BlockSpec(mix.shape, lambda j: (0, 0)),
            pl.BlockSpec((slots, block), lambda j: (0, j)),
        ]
        + [pl.BlockSpec(memory_space=pl.ANY)] * len(before),
        out_specs=pl.BlockSpec((tokens, block), lambda j: (0, first + j)),
        out_shape=jax.ShapeDtypeStruct((tokens, width), jnp.bfloat16),
        input_output_aliases={2: 0} if before else {},
        compiler_params=pltpu.CompilerParams(vmem_limit_bytes=32 * MIB),
        cost_estimate=pl.CostEstimate(
            flops=2 * slots * tokens * cols, bytes_accessed=2 * (slots + tokens) * cols, transcendentals=0
        ),
        name="combine",
    )(mix, returned, *before)


def place(index):
    dp, expert = index // 8, index % 8
    return [dp // 8, dp // 2 % 4, dp % 2, expert // 4, expert % 4]


def shift(array, axis, step):
    sizes = (2, 4, 2, 2, 4)
    pairs = []
    for source in range(128):
        at = place(source)
        for a, s in zip(axis, step):
            at[a] = (at[a] + s) % sizes[a]
        pairs.append((source, (((at[0] * 4 + at[1]) * 2 + at[2]) * 2 + at[3]) * 4 + at[4]))
    return lax.ppermute(array, AXES, pairs)


def value_weight_terms(value_input, value_grad):
    tokens, width = value_input.shape
    feats = value_grad.shape[1]
    dp, expert = lax.axis_index("dp"), lax.axis_index("expert")
    x_lo, z, core, x_hi, y = dp // 8, dp // 2 % 4, dp % 2, expert // 4, expert % 4
    parts = value_input.reshape(tokens, 2, 4, 2, 2, width // 32).transpose(3, 0, 1, 4, 2, 5)
    parts = parts.reshape(2, tokens, width // 2)
    own = jnp.where(core == 0, parts[0], parts[1])
    other = shift(jnp.where(core == 0, parts[1], parts[0]), (2,), (1,))
    other_grad = shift(value_grad, (2,), (1,))
    term = jnp.einsum("tr,tk->rk", own, value_grad, preferred_element_type=jnp.float32)
    term = term + jnp.einsum("tr,tk->rk", other, other_grad, preferred_element_type=jnp.float32)
    term = term.reshape(4, width // 8, feats)

    def pick(array, at, dim):
        return lax.dynamic_index_in_dim(array, at, dim, keepdims=False)

    total = pick(term, x_lo * 2 + x_hi, 0)
    for a, b in ((1, 0), (1, 1), (0, 1)):
        piece = pick(term, (x_lo + a) % 2 * 2 + (x_hi + b) % 2, 0).astype(jnp.bfloat16)
        total = total + shift(piece, (0, 3), (a, b)).astype(jnp.float32)
    for axis, here, lead in ((4, y, (4, 4)), (1, z, (4,))):
        term = total.reshape(*lead, -1, feats)
        dim = len(lead) - 1
        total = pick(term, here, dim)
        for k in (1, 3, 2):
            total = total + shift(pick(term, (here + k) % 4, dim), (axis,), (k,))
    return total.reshape(-1, feats)


def place(index):
    dp, expert = index // 8, index % 8
    return [dp // 8, dp // 2 % 4, dp % 2, expert // 4, expert % 4]


def shift(array, axis, step):
    sizes = (2, 4, 2, 2, 4)
    pairs = []
    for source in range(128):
        at = place(source)
        for a, s in zip(axis, step):
            at[a] = (at[a] + s) % sizes[a]
        pairs.append((source, (((at[0] * 4 + at[1]) * 2 + at[2]) * 2 + at[3]) * 4 + at[4]))
    return lax.ppermute(array, AXES, pairs)


def pick(array, at, dim):
    return lax.dynamic_index_in_dim(array, at, dim, keepdims=False)


def by_core(core, first, second):
    return jnp.where(core == 0, first, second), jnp.where(core == 0, second, first)


def body(
    value_input,
    value_grad,
    value_weight,
    out_grad,
    route_ids,
    route_slots,
    seq_lengths,
    route_weights,
    gate_act,
    up_act,
    w_gate,
    w_up,
    w_down,
):
    tokens, width = out_grad.shape
    dp = lax.axis_size("dp")
    experts = lax.axis_size("expert")
    devices = dp * experts
    capacity = gate_act.shape[2]
    ffw = gate_act.shape[3]
    slots = devices * capacity

    live = jnp.arange(tokens, dtype=jnp.int32) < seq_lengths[0]
    slot = jnp.where(live[:, None], route_ids * capacity + route_slots, -1)

    in_parts = ((0, 1024), (1024, 3072))
    dp, expert = lax.axis_index("dp"), lax.axis_index("expert")
    x_lo, z, core, x_hi, y = dp // 8, dp // 2 % 4, dp % 2, expert // 4, expert % 4
    feats = value_grad.shape[1]
    half, cols = width // 2, width // 16

    with jax.named_scope("value_first"):
        beside = shift(value_weight, (0,), (1,))

    with jax.named_scope("dispatch"):
        send = build_rows(seq_lengths, route_ids.T, route_slots.T, out_grad, slots)
        send, beside, value_in = lax.optimization_barrier((send, beside, value_input))
        routed = exchange(send.reshape(devices, capacity, width), AXES).reshape(slots, width)

    with jax.named_scope("value_second"):
        pair = jnp.stack(by_core(x_lo, value_weight, beside))
        halves = value_in.reshape(tokens, 8, 2, cols)
        own, other = by_core(core, halves[:, :, 0], halves[:, :, 1])
        other = jnp.concatenate([other.reshape(tokens, half), value_grad], axis=1)
        other = shift(other, (2,), (1,))
        inputs = jnp.concatenate([own.reshape(tokens, half), other[:, :half]])
        inputs = inputs.reshape(2 * tokens, 2, 4, 2, cols // 2)
        grads = jnp.concatenate([value_grad, other[:, half:]])

        def along_x(a, b):
            at = (0, (x_lo + a) % 2, 0, (x_hi + b) % 2, 0)
            part = lax.dynamic_slice(inputs, at, (2 * tokens, 1, 4, 1, cols // 2))
            return jnp.concatenate([part.reshape(2 * tokens, 2 * cols), grads], axis=1)

        steps = ((0, 1), (1, 0), (1, 1))
        kept = along_x(0, 0)
        packs = [along_x(*step) for step in steps]
        mix = mix_weights(slot, route_weights.astype(jnp.float32), slots)
        routed, mix, pair, kept, *packs = lax.optimization_barrier((routed, mix, pair, kept, *packs))
        below, above = shift(pair, (1,), (1,)), shift(pair, (1,), (3,))
        arrived = [shift(pack, (0, 3), step) for pack, step in zip(packs, steps)]

    with jax.named_scope("experts"):
        hidden, score = hidden_grads(
            routed, w_down[0], gate_act.reshape(slots, ffw), up_act.reshape(slots, ffw), in_parts[0][1]
        )
        slot_first = slot_grads(hidden, w_gate[0], w_up[0], *in_parts[0], score)
        slot_second = slot_grads(hidden, w_gate[0], w_up[0], *in_parts[1])

    with jax.named_scope("value_third"):
        held = lax.optimization_barrier((slot_first, below, above, *arrived))
        slot_first, below, above = held[:3]
        halfway = [shift(below[0], (1,), (1,)), shift(above[1], (1,), (3,))]
        packs = jnp.concatenate([kept, *held[3:]])
        term = jnp.einsum(
            "tr,tk->rk", packs[:, : 2 * cols], packs[:, 2 * cols :], preferred_element_type=jnp.float32
        )
        term = term.reshape(4, 4, cols // 8, feats)
        total = pick(term, y, 1)
        sent = [pick(term, (y + k) % 4, 1).astype(jnp.bfloat16) for k in (1, 2, 3)]
        terms = [shift(t, (4,), (k,)) for t, k in zip(sent, (1, 2, 3))]

    with jax.named_scope("return"):
        first = exchange(slot_first.reshape(devices, capacity, -1), AXES).reshape(slots, -1)
        held = lax.optimization_barrier((slot_second, *halfway, *terms))
        slot_second, halfway, terms = held[0], held[1:3], held[3:]
        second = exchange(slot_second.reshape(devices, capacity, -1), AXES).reshape(slots, -1)
        moe_input_grad = combine(mix, first, *in_parts[0], width)
        scores = first[:, in_parts[0][1]].astype(jnp.float32)
        weight_grad = jnp.sum(
            jnp.where(slot[:, :, None] == jnp.arange(slots, dtype=jnp.int32), scores, 0.0), axis=2
        ).astype(jnp.bfloat16)
        moe_input_grad = combine(mix, second, *in_parts[1], width, moe_input_grad)

    with jax.named_scope("value_last"):
        for part in terms:
            total = total + part.astype(jnp.float32)
        last = [shift(pick(total, (z + k) % 4, 0), (1,), (k,)) for k in (1, 2, 3)]

        ring = jnp.stack([pair, above, jnp.stack(halfway), below])
        across = shift(ring, (2,), (1,))

        def products(weight):
            out = jnp.einsum("tk,ixrk->ixtr", value_grad, weight, preferred_element_type=jnp.float32)
            out = out.astype(jnp.bfloat16)
            return lax.dynamic_slice_in_dim(jnp.concatenate([out, out]), (4 - z) % 4, 4, axis=0)

        both = jnp.stack(by_core(core, products(ring), products(across)))
        value_input_grad = both.transpose(3, 2, 1, 0, 4).reshape(tokens, width)

    with jax.named_scope("finish"):
        moe_input_grad, *last = lax.optimization_barrier((moe_input_grad, *last))
        value_weight_grad = pick(total, z, 0) + last[0] + last[1] + last[2]
    return (moe_input_grad, weight_grad, value_input_grad, value_weight_grad)


def solution(mesh):
    split = P(AXES, None)
    return jax.shard_map(
        body,
        mesh=mesh,
        in_specs=(
            split,
            split,
            P("dp", None),
            split,
            split,
            split,
            P(AXES),
            split,
            P(AXES, None, None, None),
            P(AXES, None, None, None),
            P(AXES, None, None),
            P(AXES, None, None),
            P(AXES, None, None),
        ),
        out_specs=(split, split, split, split),
        check_vma=False,
    )
```

```python
import math

import jax
import jax.numpy as jnp
from jax import lax
from jax.experimental import pallas as pl
from jax.experimental.pallas import tpu as pltpu
from jax.sharding import Mesh, PartitionSpec as P

PLACE = ("x_lo", "z", "core", "x_hi", "y")
SIZES = (2, 4, 2, 2, 4)
ORDER = ("z", "y", "x_hi", "x_lo", "core")
MIB = 1024 * 1024
LANES = 128
CAPACITY = 8
NT = (((1,), (1,)), ((), ()))


def dot_nt(left, right):
    return lax.dot_general(left, right, NT, preferred_element_type=jnp.float32)


def in_order(device):
    x_lo, z, core, x_hi, y = device // 64, device // 16 % 4, device // 8 % 2, device // 4 % 2, device % 4
    return (((z * 4 + y) * 2 + x_hi) * 2 + x_lo) * 2 + core


def exchange(array, axes):
    return lax.all_to_all(array, axes, split_axis=0, concat_axis=0, tiled=True)


def rows_kernel(length_ref, ids_ref, slots_ref, grad_ref, out_ref):
    rows, width = out_ref.shape
    top, tokens = ids_ref.shape
    live = lax.broadcasted_iota(jnp.int32, (1, tokens), 1) < length_ref[0]
    slot = lax.broadcasted_iota(jnp.int32, (rows, tokens), 0) + pl.program_id(0) * rows
    hit = None
    for k in range(top):
        name = in_order(ids_ref[k : k + 1, :]) * CAPACITY + slots_ref[k : k + 1, :]
        name = jnp.where(live, name, -1)
        hit = name == slot if hit is None else hit | (name == slot)
    pick = jnp.where(hit, 1.0, 0.0).astype(jnp.bfloat16)
    step = 1024
    for c in range(0, width, step):
        out_ref[:, c : c + step] = jnp.dot(
            pick, grad_ref[:, c : c + step], preferred_element_type=jnp.float32
        ).astype(jnp.bfloat16)


def build_rows(seq_lengths, ids_t, slots_t, out_grad, slots):
    tokens, width = out_grad.shape
    rows = 256
    return pl.pallas_call(
        rows_kernel,
        grid=(slots // rows,),
        in_specs=[
            pl.BlockSpec(memory_space=pltpu.SMEM),
            pl.BlockSpec(ids_t.shape, lambda i: (0, 0)),
            pl.BlockSpec(slots_t.shape, lambda i: (0, 0)),
            pl.BlockSpec((tokens, width), lambda i: (0, 0)),
        ],
        out_specs=pl.BlockSpec((rows, width), lambda i: (i, 0)),
        out_shape=pltpu.HBM((slots, width), jnp.bfloat16),
        compiler_params=pltpu.CompilerParams(vmem_limit_bytes=32 * MIB),
        cost_estimate=pl.CostEstimate(
            flops=2 * slots * tokens * width, bytes_accessed=2 * (slots + tokens) * width, transcendentals=0
        ),
        name="build_rows",
    )(seq_lengths, *[pltpu.with_memory_space_constraint(a, pltpu.HBM) for a in (ids_t, slots_t, out_grad)])


def hidden_kernel(x_ref, down_ref, gate_ref, up_ref, hidden_ref, score_ref):
    rows = x_ref.shape[0]
    ffw = down_ref.shape[0]
    part = 256
    score = jnp.zeros((rows, LANES), jnp.float32)
    for c in range(0, ffw, part):
        cols = slice(c, c + part)
        back = dot_nt(x_ref[...], down_ref[cols, :])
        gate = gate_ref[:, cols].astype(jnp.float32)
        up = up_ref[:, cols].astype(jnp.float32)
        sig = 1.0 / (1.0 + jnp.exp(-gate))
        up_grad = back * (gate * sig)
        hidden_ref[:, ffw + c : ffw + c + part] = up_grad.astype(jnp.bfloat16)
        hidden_ref[:, cols] = (back * up * sig * (1.0 + gate * (1.0 - sig))).astype(jnp.bfloat16)
        term = up_grad * up
        for lane in range(0, part, LANES):
            score = score + term[:, lane : lane + LANES]
    score = jnp.sum(score, axis=1, keepdims=True)
    score_ref[...] = jnp.broadcast_to(score, score_ref.shape).astype(jnp.bfloat16)


def hidden_grads(rows_in, down, gate, up, score_at):
    slots, width = rows_in.shape
    ffw = down.shape[0]
    rows = 256
    return pl.pallas_call(
        hidden_kernel,
        grid=(slots // rows,),
        in_specs=[
            pl.BlockSpec((rows, width), lambda i: (i, 0)),
            pl.BlockSpec(memory_space=pltpu.VMEM),
            pl.BlockSpec((rows, ffw), lambda i: (i, 0)),
            pl.BlockSpec((rows, ffw), lambda i: (i, 0)),
        ],
        out_specs=[
            pl.BlockSpec((rows, 2 * ffw), lambda i: (i, 0)),
            pl.BlockSpec((rows, LANES), lambda i: (i, score_at // LANES)),
        ],
        out_shape=[
            jax.ShapeDtypeStruct((slots, 2 * ffw), jnp.bfloat16),
            pltpu.HBM((slots, score_at + LANES), jnp.bfloat16),
        ],
        compiler_params=pltpu.CompilerParams(vmem_limit_bytes=32 * MIB),
        cost_estimate=pl.CostEstimate(flops=1, bytes_accessed=1, transcendentals=0),
        name="hidden_grads",
    )(
        rows_in,
        pltpu.with_memory_space_constraint(down, pltpu.VMEM),
        pltpu.with_memory_space_constraint(gate, pltpu.HBM),
        pltpu.with_memory_space_constraint(up, pltpu.HBM),
    )


def slot_kernel(hidden_ref, gate_w_ref, up_w_ref, *refs):
    out_ref = refs[-1]
    ffw = gate_w_ref.shape[1]
    part = 256
    for r in range(0, out_ref.shape[0], part):
        here = slice(r, r + part)
        out_ref[here, :] = (
            dot_nt(hidden_ref[here, :ffw], gate_w_ref[...]) + dot_nt(hidden_ref[here, ffw:], up_w_ref[...])
        ).astype(jnp.bfloat16)


def slot_grads(hidden, gate_w, up_w, start, width, into=None):
    slots = hidden.shape[0]
    ffw = gate_w.shape[1]
    block = 512
    first = start // block
    before = () if into is None else (into,)
    cost = pl.CostEstimate(flops=1, bytes_accessed=1, transcendentals=0)
    if into is None:
        cost = pl.CostEstimate(
            flops=4 * slots * width * ffw,
            bytes_accessed=2 * (slots * width + 2 * ffw * width + 2 * slots * ffw),
            transcendentals=0,
        )
    return pl.pallas_call(
        slot_kernel,
        grid=(width // block,),
        in_specs=[
            pl.BlockSpec((slots, 2 * ffw), lambda j: (0, 0)),
            pl.BlockSpec((block, ffw), lambda j: (first + j, 0)),
            pl.BlockSpec((block, ffw), lambda j: (first + j, 0)),
        ]
        + [pl.BlockSpec(memory_space=pl.ANY)] * len(before),
        out_specs=pl.BlockSpec((slots, block), lambda j: (0, j)),
        out_shape=pltpu.HBM((slots, width if into is None else into.shape[1]), jnp.bfloat16),
        input_output_aliases={3: 0} if before else {},
        compiler_params=pltpu.CompilerParams(vmem_limit_bytes=32 * MIB),
        cost_estimate=cost,
        name="slot_grads",
    )(
        hidden,
        pltpu.with_memory_space_constraint(gate_w, pltpu.HBM),
        pltpu.with_memory_space_constraint(up_w, pltpu.HBM),
        *before,
    )


def mix_kernel(slot_ref, weight_ref, mix_ref):
    slot = lax.broadcasted_iota(jnp.int32, mix_ref.shape, 1)
    mix = jnp.zeros(mix_ref.shape, jnp.float32)
    for k in range(slot_ref.shape[1]):
        mix = mix + jnp.where(slot_ref[:, k : k + 1] == slot, weight_ref[:, k : k + 1], 0.0)
    mix_ref[...] = mix.astype(jnp.bfloat16)


def mix_weights(slot, weight, slots):
    return pl.pallas_call(
        mix_kernel,
        out_shape=jax.ShapeDtypeStruct((slot.shape[0], slots), jnp.bfloat16),
        name="mix_weights",
    )(slot, weight)


def combine_kernel(mix_ref, rows_ref, *refs):
    refs[-1][...] = jnp.dot(mix_ref[...], rows_ref[...], preferred_element_type=jnp.float32).astype(jnp.bfloat16)


def combine(mix, returned, start, cols, width, earlier=None):
    slots = returned.shape[0]
    tokens = mix.shape[0]
    block = 1024
    first = start // block
    before = () if earlier is None else (earlier,)
    return pl.pallas_call(
        combine_kernel,
        grid=(cols // block,),
        in_specs=[
            pl.BlockSpec(mix.shape, lambda j: (0, 0)),
            pl.BlockSpec((slots, block), lambda j: (0, j)),
        ]
        + [pl.BlockSpec(memory_space=pl.ANY)] * len(before),
        out_specs=pl.BlockSpec((tokens, block), lambda j: (0, first + j)),
        out_shape=jax.ShapeDtypeStruct((tokens, width), jnp.bfloat16),
        input_output_aliases={2: 0} if before else {},
        compiler_params=pltpu.CompilerParams(vmem_limit_bytes=32 * MIB),
        cost_estimate=pl.CostEstimate(
            flops=2 * slots * tokens * cols, bytes_accessed=2 * (slots + tokens) * cols, transcendentals=0
        ),
        name="combine",
    )(mix, returned, *before)


def term_kernel(place_ref, *refs):
    packs, (own_ref, *sent_refs), term_ref = refs[:4], refs[4:8], refs[8]
    cols = packs[0].shape[1] // 2
    term = None
    for pack in packs:
        one = lax.dot_general(
            pack[:, :cols], pack[:, cols:], (((0,), (0,)), ((), ())), preferred_element_type=jnp.float32
        )
        term = one if term is None else term + one
    term_ref[...] = term
    rows = cols // 16
    for k, out_ref in enumerate((own_ref, *sent_refs)):
        at = lax.rem(place_ref[0] + k, 4)
        for z in range(4):
            start = pl.multiple_of(z * 4 * rows + at * rows, rows)
            out_ref[z * rows : (z + 1) * rows, :] = term_ref[pl.ds(start, rows), :].astype(out_ref.dtype)


def split_terms(place, packs):
    cols = packs[0].shape[1] // 2
    shape = (cols // 4, cols)
    return pl.pallas_call(
        term_kernel,
        in_specs=[pl.BlockSpec(memory_space=pltpu.SMEM)] + [pl.BlockSpec(memory_space=pltpu.VMEM)] * 4,
        out_specs=[pl.BlockSpec(memory_space=pltpu.VMEM)] * 4,
        out_shape=[jax.ShapeDtypeStruct(shape, jnp.float32)] + [jax.ShapeDtypeStruct(shape, jnp.bfloat16)] * 3,
        scratch_shapes=[pltpu.VMEM((cols, cols), jnp.float32)],
        compiler_params=pltpu.CompilerParams(vmem_limit_bytes=16 * MIB),
        cost_estimate=pl.CostEstimate(flops=1, bytes_accessed=1, transcendentals=0),
        name="split_terms",
    )(place, *packs)


def shift(array, axes, steps):
    sizes = [lax.axis_size(axis) for axis in axes]
    pairs = []
    for source in range(math.prod(sizes)):
        target, rest, scale = 0, source, 1
        for size, step in zip(reversed(sizes), reversed(steps)):
            target += (rest % size + step) % size * scale
            rest, scale = rest // size, scale * size
        pairs.append((source, target))
    return lax.ppermute(array, axes, pairs)


def pick(array, at, dim):
    return lax.dynamic_index_in_dim(array, at, dim, keepdims=False)


def by_core(core, first, second):
    return jnp.where(core == 0, first, second), jnp.where(core == 0, second, first)


def body(
    value_input,
    value_grad,
    value_weight,
    out_grad,
    route_ids,
    route_slots,
    seq_lengths,
    route_weights,
    gate_act,
    up_act,
    w_gate,
    w_up,
    w_down,
):
    tokens, width = out_grad.shape
    feats = value_grad.shape[1]
    devices, capacity, ffw = gate_act.shape[1:]
    slots = devices * capacity
    x_lo, z, core, x_hi, y = (lax.axis_index(axis) for axis in PLACE)
    half, cols = width // 2, width // 16
    in_parts = ((0, 1024), (1024, 3072))

    live = jnp.arange(tokens, dtype=jnp.int32) < seq_lengths[0]
    slot = jnp.where(live[:, None], in_order(route_ids) * capacity + route_slots, -1)

    with jax.named_scope("value_first"):
        beside = shift(value_weight, ("x_lo",), (1,))

    with jax.named_scope("dispatch"):
        send = build_rows(seq_lengths, route_ids.T, route_slots.T, out_grad, slots)
        send, beside, value_in, gate_act, up_act = lax.optimization_barrier(
            (send, beside, value_input, gate_act, up_act)
        )
        routed = exchange(send.reshape(devices, capacity, width), ORDER).reshape(slots, width)

    with jax.named_scope("value_second"):
        pair = jnp.stack(by_core(x_lo, value_weight, beside))
        halves = value_in.reshape(tokens, 8, 2, cols)
        own, other = by_core(core, halves[:, :, 0], halves[:, :, 1])
        other = jnp.concatenate([other.reshape(tokens, half), value_grad], axis=1)
        other = shift(other, ("core",), (1,))
        inputs = jnp.concatenate([own.reshape(tokens, half), other[:, :half]])
        inputs = inputs.reshape(2 * tokens, 2, 4, 2, cols // 2)
        grads = jnp.concatenate([value_grad, other[:, half:]])

        def along_x(a, b):
            at = (0, (x_lo + a) % 2, 0, (x_hi + b) % 2, 0)
            part = lax.dynamic_slice(inputs, at, (2 * tokens, 1, 4, 1, cols // 2))
            return jnp.concatenate([part.reshape(2 * tokens, 2 * cols), grads], axis=1)

        steps = ((0, 1), (1, 0), (1, 1))
        kept = along_x(0, 0)
        packs = [along_x(*step) for step in steps]
        mix = mix_weights(slot, route_weights.astype(jnp.float32), slots)
        gate_act, up_act = (
            a.reshape(*SIZES, capacity, ffw).transpose(1, 4, 3, 0, 2, 5, 6).reshape(slots, ffw)
            for a in (gate_act, up_act)
        )
        routed, mix, pair, kept, gate_act, up_act, *packs = lax.optimization_barrier(
            (routed, mix, pair, kept, gate_act, up_act, *packs)
        )
        below, above = shift(pair, ("z",), (1,)), shift(pair, ("z",), (3,))
        arrived = [shift(pack, ("x_lo", "x_hi"), step) for pack, step in zip(packs, steps)]

    with jax.named_scope("experts"):
        hidden, score = hidden_grads(routed, w_down[0], gate_act, up_act, in_parts[0][1])
        slot_first = slot_grads(hidden, w_gate[0], w_up[0], *in_parts[0], score)
        slot_second = slot_grads(hidden, w_gate[0], w_up[0], *in_parts[1])

    with jax.named_scope("value_third"):
        held = lax.optimization_barrier((slot_first, below, above, *arrived))
        slot_first, below, above = held[:3]
        total, *sent = split_terms(y.reshape(1), (kept, *held[3:]))
        terms = [shift(t, ("y",), (k,)) for t, k in zip(sent, (1, 2, 3))]
        halfway = [shift(below[0], ("z",), (1,)), shift(above[1], ("z",), (3,))]

    with jax.named_scope("return"):
        first = exchange(slot_first.reshape(devices, capacity, -1), ORDER).reshape(slots, -1)
        held = lax.optimization_barrier((slot_second, *halfway, *terms))
        slot_second, halfway, terms = held[0], held[1:3], held[3:]
        second = exchange(slot_second.reshape(devices, capacity, -1), ORDER).reshape(slots, -1)
        moe_input_grad = combine(mix, first, *in_parts[0], width)
        scores = first[:, in_parts[0][1]].astype(jnp.float32)
        weight_grad = jnp.sum(
            jnp.where(slot[:, :, None] == jnp.arange(slots, dtype=jnp.int32), scores, 0.0), axis=2
        ).astype(jnp.bfloat16)
        moe_input_grad = combine(mix, second, *in_parts[1], width, moe_input_grad)

    with jax.named_scope("value_last"):
        for part in terms:
            total = total + part.astype(jnp.float32)
        total = total.reshape(4, cols // 8, feats)
        last = [shift(pick(total, (z + k) % 4, 0), ("z",), (k,)) for k in (1, 2, 3)]
        total = pick(total, z, 0)

        ring = jnp.stack([pair, above, jnp.stack(halfway), below])
        across = shift(ring, ("core",), (1,))

        def products(weight):
            out = jnp.einsum("tk,ixrk->ixtr", value_grad, weight, preferred_element_type=jnp.float32)
            out = out.astype(jnp.bfloat16)
            return lax.dynamic_slice_in_dim(jnp.concatenate([out, out]), (4 - z) % 4, 4, axis=0)

        both = jnp.stack(by_core(core, products(ring), products(across)))
        value_input_grad = both.transpose(3, 2, 1, 0, 4).reshape(tokens, width)

    with jax.named_scope("finish"):
        moe_input_grad, *last = lax.optimization_barrier((moe_input_grad, *last))
        value_weight_grad = total + last[0] + last[1] + last[2]
    return (moe_input_grad, weight_grad, value_input_grad, value_weight_grad)


def solution(mesh):
    places = Mesh(mesh.devices.reshape(SIZES), PLACE)
    split = P(PLACE, None)
    return jax.shard_map(
        body,
        mesh=places,
        in_specs=(
            split,
            split,
            P(PLACE[:3], None),
            split,
            split,
            split,
            P(PLACE),
            split,
            P(PLACE, None, None, None),
            P(PLACE, None, None, None),
            P(PLACE, None, None),
            P(PLACE, None, None),
            P(PLACE, None, None),
        ),
        out_specs=(split, split, split, split),
        check_vma=False,
    )
```

```python
import math

import jax
import jax.numpy as jnp
from jax import lax
from jax.experimental import pallas as pl
from jax.experimental.pallas import tpu as pltpu
from jax.sharding import Mesh, PartitionSpec as P

PLACE = ("x_lo", "z", "core", "x_hi", "y")
SIZES = (2, 4, 2, 2, 4)
ORDER = ("z", "y", "x_hi", "x_lo", "core")
MIB = 1024 * 1024
LANES = 128
CAPACITY = 8
NT = (((1,), (1,)), ((), ()))


def dot_nt(left, right):
    return lax.dot_general(left, right, NT, preferred_element_type=jnp.float32)


def in_order(device):
    x_lo, z, core, x_hi, y = device // 64, device // 16 % 4, device // 8 % 2, device // 4 % 2, device % 4
    return (((z * 4 + y) * 2 + x_hi) * 2 + x_lo) * 2 + core


def exchange(array, axes):
    return lax.all_to_all(array, axes, split_axis=0, concat_axis=0, tiled=True)


def rows_kernel(length_ref, ids_ref, slots_ref, grad_ref, out_ref):
    rows, width = out_ref.shape
    top, tokens = ids_ref.shape
    live = lax.broadcasted_iota(jnp.int32, (1, tokens), 1) < length_ref[0]
    slot = lax.broadcasted_iota(jnp.int32, (rows, tokens), 0) + pl.program_id(0) * rows
    hit = None
    for k in range(top):
        name = in_order(ids_ref[k : k + 1, :]) * CAPACITY + slots_ref[k : k + 1, :]
        name = jnp.where(live, name, -1)
        hit = name == slot if hit is None else hit | (name == slot)
    pick = jnp.where(hit, 1.0, 0.0).astype(jnp.bfloat16)
    step = 1024
    for c in range(0, width, step):
        out_ref[:, c : c + step] = jnp.dot(
            pick, grad_ref[:, c : c + step], preferred_element_type=jnp.float32
        ).astype(jnp.bfloat16)


def build_rows(seq_lengths, ids_t, slots_t, out_grad, slots):
    tokens, width = out_grad.shape
    rows = 256
    return pl.pallas_call(
        rows_kernel,
        grid=(slots // rows,),
        in_specs=[
            pl.BlockSpec(memory_space=pltpu.SMEM),
            pl.BlockSpec(ids_t.shape, lambda i: (0, 0)),
            pl.BlockSpec(slots_t.shape, lambda i: (0, 0)),
            pl.BlockSpec((tokens, width), lambda i: (0, 0)),
        ],
        out_specs=pl.BlockSpec((rows, width), lambda i: (i, 0)),
        out_shape=pltpu.HBM((slots, width), jnp.bfloat16),
        compiler_params=pltpu.CompilerParams(vmem_limit_bytes=32 * MIB),
        cost_estimate=pl.CostEstimate(
            flops=2 * slots * tokens * width, bytes_accessed=2 * (slots + tokens) * width, transcendentals=0
        ),
        name="build_rows",
    )(seq_lengths, *[pltpu.with_memory_space_constraint(a, pltpu.HBM) for a in (ids_t, slots_t, out_grad)])


def hidden_kernel(x_ref, down_ref, gate_ref, up_ref, hidden_ref, score_ref):
    rows = x_ref.shape[0]
    ffw = down_ref.shape[0]
    part = 256
    score = jnp.zeros((rows, LANES), jnp.float32)
    for c in range(0, ffw, part):
        cols = slice(c, c + part)
        back = dot_nt(x_ref[...], down_ref[cols, :])
        gate = gate_ref[:, cols].astype(jnp.float32)
        up = up_ref[:, cols].astype(jnp.float32)
        sig = 1.0 / (1.0 + jnp.exp(-gate))
        up_grad = back * (gate * sig)
        hidden_ref[:, ffw + c : ffw + c + part] = up_grad.astype(jnp.bfloat16)
        hidden_ref[:, cols] = (back * up * sig * (1.0 + gate * (1.0 - sig))).astype(jnp.bfloat16)
        term = up_grad * up
        for lane in range(0, part, LANES):
            score = score + term[:, lane : lane + LANES]
    score = jnp.sum(score, axis=1, keepdims=True)
    score_ref[...] = jnp.broadcast_to(score, score_ref.shape).astype(jnp.bfloat16)


def hidden_grads(rows_in, down, gate, up, score_at):
    slots, width = rows_in.shape
    ffw = down.shape[0]
    rows = 256
    return pl.pallas_call(
        hidden_kernel,
        grid=(slots // rows,),
        in_specs=[
            pl.BlockSpec((rows, width), lambda i: (i, 0)),
            pl.BlockSpec(memory_space=pltpu.VMEM),
            pl.BlockSpec((rows, ffw), lambda i: (i, 0)),
            pl.BlockSpec((rows, ffw), lambda i: (i, 0)),
        ],
        out_specs=[
            pl.BlockSpec((rows, 2 * ffw), lambda i: (i, 0)),
            pl.BlockSpec((rows, LANES), lambda i: (i, score_at // LANES)),
        ],
        out_shape=[
            jax.ShapeDtypeStruct((slots, 2 * ffw), jnp.bfloat16),
            pltpu.HBM((slots, score_at + LANES), jnp.bfloat16),
        ],
        compiler_params=pltpu.CompilerParams(vmem_limit_bytes=32 * MIB),
        cost_estimate=pl.CostEstimate(flops=1, bytes_accessed=1, transcendentals=0),
        name="hidden_grads",
    )(
        rows_in,
        pltpu.with_memory_space_constraint(down, pltpu.VMEM),
        pltpu.with_memory_space_constraint(gate, pltpu.HBM),
        pltpu.with_memory_space_constraint(up, pltpu.HBM),
    )


def slot_kernel(hidden_ref, gate_w_ref, up_w_ref, *refs):
    out_ref = refs[-1]
    ffw = gate_w_ref.shape[1]
    part = 256
    for r in range(0, out_ref.shape[0], part):
        here = slice(r, r + part)
        out_ref[here, :] = (
            dot_nt(hidden_ref[here, :ffw], gate_w_ref[...]) + dot_nt(hidden_ref[here, ffw:], up_w_ref[...])
        ).astype(jnp.bfloat16)


def slot_grads(hidden, gate_w, up_w, start, width, into=None):
    slots = hidden.shape[0]
    ffw = gate_w.shape[1]
    block = 512
    first = start // block
    before = () if into is None else (into,)
    cost = pl.CostEstimate(flops=1, bytes_accessed=1, transcendentals=0)
    if into is None:
        cost = pl.CostEstimate(
            flops=4 * slots * width * ffw,
            bytes_accessed=2 * (slots * width + 2 * ffw * width + 2 * slots * ffw),
            transcendentals=0,
        )
    return pl.pallas_call(
        slot_kernel,
        grid=(width // block,),
        in_specs=[
            pl.BlockSpec((slots, 2 * ffw), lambda j: (0, 0)),
            pl.BlockSpec((block, ffw), lambda j: (first + j, 0)),
            pl.BlockSpec((block, ffw), lambda j: (first + j, 0)),
        ]
        + [pl.BlockSpec(memory_space=pl.ANY)] * len(before),
        out_specs=pl.BlockSpec((slots, block), lambda j: (0, j)),
        out_shape=pltpu.HBM((slots, width if into is None else into.shape[1]), jnp.bfloat16),
        input_output_aliases={3: 0} if before else {},
        compiler_params=pltpu.CompilerParams(vmem_limit_bytes=32 * MIB),
        cost_estimate=cost,
        name="slot_grads",
    )(
        hidden,
        pltpu.with_memory_space_constraint(gate_w, pltpu.HBM),
        pltpu.with_memory_space_constraint(up_w, pltpu.HBM),
        *before,
    )


def mix_kernel(slot_ref, weight_ref, mix_ref):
    slot = lax.broadcasted_iota(jnp.int32, mix_ref.shape, 1)
    mix = jnp.zeros(mix_ref.shape, jnp.float32)
    for k in range(slot_ref.shape[1]):
        mix = mix + jnp.where(slot_ref[:, k : k + 1] == slot, weight_ref[:, k : k + 1], 0.0)
    mix_ref[...] = mix.astype(jnp.bfloat16)


def mix_weights(slot, weight, slots):
    return pl.pallas_call(
        mix_kernel,
        out_shape=jax.ShapeDtypeStruct((slot.shape[0], slots), jnp.bfloat16),
        name="mix_weights",
    )(slot, weight)


def combine_kernel(mix_ref, rows_ref, *refs):
    refs[-1][...] = jnp.dot(mix_ref[...], rows_ref[...], preferred_element_type=jnp.float32).astype(jnp.bfloat16)


def combine(mix, returned, start, cols, width, earlier=None):
    slots = returned.shape[0]
    tokens = mix.shape[0]
    block = 1024
    first = start // block
    before = () if earlier is None else (earlier,)
    return pl.pallas_call(
        combine_kernel,
        grid=(cols // block,),
        in_specs=[
            pl.BlockSpec(mix.shape, lambda j: (0, 0)),
            pl.BlockSpec((slots, block), lambda j: (0, j)),
        ]
        + [pl.BlockSpec(memory_space=pl.ANY)] * len(before),
        out_specs=pl.BlockSpec((tokens, block), lambda j: (0, first + j)),
        out_shape=jax.ShapeDtypeStruct((tokens, width), jnp.bfloat16),
        input_output_aliases={2: 0} if before else {},
        compiler_params=pltpu.CompilerParams(vmem_limit_bytes=32 * MIB),
        cost_estimate=pl.CostEstimate(
            flops=10**12 if earlier is None else 2 * slots * tokens * cols,
            bytes_accessed=2 * (slots + tokens) * cols,
            transcendentals=0,
        ),
        name="combine",
    )(mix, returned, *before)


def term_kernel(place_ref, *refs):
    packs, (own_ref, *sent_refs), term_ref = refs[:4], refs[4:8], refs[8]
    cols = packs[0].shape[1] // 2
    term = None
    for pack in packs:
        one = lax.dot_general(
            pack[:, :cols], pack[:, cols:], (((0,), (0,)), ((), ())), preferred_element_type=jnp.float32
        )
        term = one if term is None else term + one
    term_ref[...] = term
    rows = cols // 16
    for k, out_ref in enumerate((own_ref, *sent_refs)):
        at = lax.rem(place_ref[0] + k, 4)
        for z in range(4):
            start = pl.multiple_of(z * 4 * rows + at * rows, rows)
            out_ref[z * rows : (z + 1) * rows, :] = term_ref[pl.ds(start, rows), :].astype(out_ref.dtype)


def split_terms(place, packs):
    cols = packs[0].shape[1] // 2
    shape = (cols // 4, cols)
    return pl.pallas_call(
        term_kernel,
        in_specs=[pl.BlockSpec(memory_space=pltpu.SMEM)] + [pl.BlockSpec(memory_space=pltpu.VMEM)] * 4,
        out_specs=[pl.BlockSpec(memory_space=pltpu.VMEM)] * 4,
        out_shape=[jax.ShapeDtypeStruct(shape, jnp.float32)] + [jax.ShapeDtypeStruct(shape, jnp.bfloat16)] * 3,
        scratch_shapes=[pltpu.VMEM((cols, cols), jnp.float32)],
        compiler_params=pltpu.CompilerParams(vmem_limit_bytes=16 * MIB),
        cost_estimate=pl.CostEstimate(flops=1, bytes_accessed=1, transcendentals=0),
        name="split_terms",
    )(place, *packs)


def shift(array, axes, steps):
    sizes = [lax.axis_size(axis) for axis in axes]
    pairs = []
    for source in range(math.prod(sizes)):
        target, rest, scale = 0, source, 1
        for size, step in zip(reversed(sizes), reversed(steps)):
            target += (rest % size + step) % size * scale
            rest, scale = rest // size, scale * size
        pairs.append((source, target))
    return lax.ppermute(array, axes, pairs)


def pick(array, at, dim):
    return lax.dynamic_index_in_dim(array, at, dim, keepdims=False)


def by_core(core, first, second):
    return jnp.where(core == 0, first, second), jnp.where(core == 0, second, first)


def body(
    value_input,
    value_grad,
    value_weight,
    out_grad,
    route_ids,
    route_slots,
    seq_lengths,
    route_weights,
    gate_act,
    up_act,
    w_gate,
    w_up,
    w_down,
):
    tokens, width = out_grad.shape
    feats = value_grad.shape[1]
    devices, capacity, ffw = gate_act.shape[1:]
    slots = devices * capacity
    x_lo, z, core, x_hi, y = (lax.axis_index(axis) for axis in PLACE)
    half, cols = width // 2, width // 16
    in_parts = ((0, 1024), (1024, 3072))

    live = jnp.arange(tokens, dtype=jnp.int32) < seq_lengths[0]
    slot = jnp.where(live[:, None], in_order(route_ids) * capacity + route_slots, -1)

    with jax.named_scope("value_first"):
        beside = shift(value_weight, ("x_lo",), (1,))

    with jax.named_scope("dispatch"):
        send = build_rows(seq_lengths, route_ids.T, route_slots.T, out_grad, slots)
        send, beside, value_in, gate_act, up_act = lax.optimization_barrier(
            (send, beside, value_input, gate_act, up_act)
        )
        routed = exchange(send.reshape(devices, capacity, width), ORDER).reshape(slots, width)

    with jax.named_scope("value_second"):
        pair = jnp.stack(by_core(x_lo, value_weight, beside))
        halves = value_in.reshape(tokens, 8, 2, cols)
        own, other = by_core(core, halves[:, :, 0], halves[:, :, 1])
        other = jnp.concatenate([other.reshape(tokens, half), value_grad], axis=1)
        other = shift(other, ("core",), (1,))
        inputs = jnp.concatenate([own.reshape(tokens, half), other[:, :half]])
        inputs = inputs.reshape(2 * tokens, 2, 4, 2, cols // 2)
        grads = jnp.concatenate([value_grad, other[:, half:]])

        def along_x(a, b):
            at = (0, (x_lo + a) % 2, 0, (x_hi + b) % 2, 0)
            part = lax.dynamic_slice(inputs, at, (2 * tokens, 1, 4, 1, cols // 2))
            return jnp.concatenate([part.reshape(2 * tokens, 2 * cols), grads], axis=1)

        steps = ((0, 1), (1, 0), (1, 1))
        kept = along_x(0, 0)
        packs = [along_x(*step) for step in steps]
        mix = mix_weights(slot, route_weights.astype(jnp.float32), slots)
        gate_act, up_act = (
            a.reshape(*SIZES, capacity, ffw).transpose(1, 4, 3, 0, 2, 5, 6).reshape(slots, ffw)
            for a in (gate_act, up_act)
        )
        below, above = shift(pair, ("z",), (1,)), shift(pair, ("z",), (3,))
        arrived = [shift(pack, ("x_lo", "x_hi"), step) for pack, step in zip(packs, steps)]
        routed, mix, kept, gate_act, up_act, *_ = lax.optimization_barrier(
            (routed, mix, kept, gate_act, up_act, pair, *packs)
        )

    with jax.named_scope("experts"):
        hidden, score = hidden_grads(routed, w_down[0], gate_act, up_act, in_parts[0][1])
        slot_first = slot_grads(hidden, w_gate[0], w_up[0], *in_parts[0], score)
        slot_second = slot_grads(hidden, w_gate[0], w_up[0], *in_parts[1])

    with jax.named_scope("value_third"):
        held = lax.optimization_barrier((slot_first, below, above, *arrived))
        slot_first, below, above = held[:3]
        total, *sent = split_terms(y.reshape(1), (kept, *held[3:]))
        terms = [shift(t, ("y",), (k,)) for t, k in zip(sent, (1, 2, 3))]
        halfway = [shift(below[0], ("z",), (1,)), shift(above[1], ("z",), (3,))]

    with jax.named_scope("return"):
        first = exchange(slot_first.reshape(devices, capacity, -1), ORDER).reshape(slots, -1)
        second = exchange(slot_second.reshape(devices, capacity, -1), ORDER).reshape(slots, -1)
        moe_input_grad = combine(mix, first, *in_parts[0], width)
        moe_input_grad, *held = lax.optimization_barrier((moe_input_grad, *halfway, *terms))
        halfway, terms = held[:2], held[2:]
        scores = first[:, in_parts[0][1]].astype(jnp.float32)
        weight_grad = jnp.sum(
            jnp.where(slot[:, :, None] == jnp.arange(slots, dtype=jnp.int32), scores, 0.0), axis=2
        ).astype(jnp.bfloat16)
        moe_input_grad = combine(mix, second, *in_parts[1], width, moe_input_grad)

    with jax.named_scope("value_last"):
        for part in terms:
            total = total + part.astype(jnp.float32)
        total = total.reshape(4, cols // 8, feats)
        last = [shift(pick(total, (z + k) % 4, 0), ("z",), (k,)) for k in (1, 2, 3)]
        total = pick(total, z, 0)

        ring = jnp.stack([pair, above, jnp.stack(halfway), below])
        across = shift(ring, ("core",), (1,))

        def products(weight):
            out = jnp.einsum("tk,ixrk->ixtr", value_grad, weight, preferred_element_type=jnp.float32)
            out = out.astype(jnp.bfloat16)
            return lax.dynamic_slice_in_dim(jnp.concatenate([out, out]), (4 - z) % 4, 4, axis=0)

        both = jnp.stack(by_core(core, products(ring), products(across)))
        value_input_grad = both.transpose(3, 2, 1, 0, 4).reshape(tokens, width)

    with jax.named_scope("finish"):
        moe_input_grad, total, *last = lax.optimization_barrier((moe_input_grad, total, *last))
        value_weight_grad = total + last[0] + last[1] + last[2]
    return (moe_input_grad, weight_grad, value_input_grad, value_weight_grad)


def solution(mesh):
    places = Mesh(mesh.devices.reshape(SIZES), PLACE)
    split = P(PLACE, None)
    return jax.shard_map(
        body,
        mesh=places,
        in_specs=(
            split,
            split,
            P(PLACE[:3], None),
            split,
            split,
            split,
            P(PLACE),
            split,
            P(PLACE, None, None, None),
            P(PLACE, None, None, None),
            P(PLACE, None, None),
            P(PLACE, None, None),
            P(PLACE, None, None),
        ),
        out_specs=(split, split, split, split),
        check_vma=False,
    )
```

```python
import math

import jax
import jax.numpy as jnp
from jax import lax
from jax.experimental import pallas as pl
from jax.experimental.pallas import tpu as pltpu
from jax.sharding import Mesh, PartitionSpec as P

PLACE = ("x_lo", "z", "core", "x_hi", "y")
SIZES = (2, 4, 2, 2, 4)
ORDER = ("z", "y", "x_hi", "core", "x_lo")
MIB = 1024 * 1024
LANES = 128
CAPACITY = 8
NT = (((1,), (1,)), ((), ()))


def dot_nt(left, right):
    return lax.dot_general(left, right, NT, preferred_element_type=jnp.float32)


def in_order(device):
    x_lo, z, core, x_hi, y = device // 64, device // 16 % 4, device // 8 % 2, device // 4 % 2, device % 4
    return (((z * 4 + y) * 2 + x_hi) * 2 + core) * 2 + x_lo


def exchange(array, axes):
    return lax.all_to_all(array, axes, split_axis=0, concat_axis=0, tiled=True)


def rows_kernel(length_ref, ids_ref, slots_ref, grad_ref, out_ref):
    rows, width = out_ref.shape
    top, tokens = ids_ref.shape
    live = lax.broadcasted_iota(jnp.int32, (1, tokens), 1) < length_ref[0]
    slot = lax.broadcasted_iota(jnp.int32, (rows, tokens), 0) + pl.program_id(0) * rows
    hit = None
    for k in range(top):
        name = in_order(ids_ref[k : k + 1, :]) * CAPACITY + slots_ref[k : k + 1, :]
        name = jnp.where(live, name, -1)
        hit = name == slot if hit is None else hit | (name == slot)
    pick = jnp.where(hit, 1.0, 0.0).astype(jnp.bfloat16)
    step = 1024
    for c in range(0, width, step):
        out_ref[:, c : c + step] = jnp.dot(
            pick, grad_ref[:, c : c + step], preferred_element_type=jnp.float32
        ).astype(jnp.bfloat16)


def build_rows(seq_lengths, ids_t, slots_t, out_grad, slots):
    tokens, width = out_grad.shape
    rows = 256
    return pl.pallas_call(
        rows_kernel,
        grid=(slots // rows,),
        in_specs=[
            pl.BlockSpec(memory_space=pltpu.SMEM),
            pl.BlockSpec(ids_t.shape, lambda i: (0, 0)),
            pl.BlockSpec(slots_t.shape, lambda i: (0, 0)),
            pl.BlockSpec((tokens, width), lambda i: (0, 0)),
        ],
        out_specs=pl.BlockSpec((rows, width), lambda i: (i, 0)),
        out_shape=pltpu.HBM((slots, width), jnp.bfloat16),
        compiler_params=pltpu.CompilerParams(vmem_limit_bytes=32 * MIB),
        cost_estimate=pl.CostEstimate(
            flops=2 * slots * tokens * width, bytes_accessed=2 * (slots + tokens) * width, transcendentals=0
        ),
        name="build_rows",
    )(seq_lengths, *[pltpu.with_memory_space_constraint(a, pltpu.HBM) for a in (ids_t, slots_t, out_grad)])


def hidden_kernel(x_ref, down_ref, gate_hbm, up_hbm, hidden_ref, score_ref, back_ref, gate_ref, up_ref, sems):
    k = pl.program_id(0)
    last = pl.num_programs(0) - 1
    rows, ffw = back_ref.shape
    part = 256
    copies = [
        pltpu.make_async_copy(gate_hbm, gate_ref, sems.at[0]),
        pltpu.make_async_copy(up_hbm, up_ref, sems.at[1]),
    ]

    @pl.when(k == 0)
    def _():
        for copy in copies:
            copy.start()
        for r in range(0, rows, part):
            back_ref[r : r + part, :] = dot_nt(x_ref[r : r + part, :], down_ref[...])

    @pl.when(jnp.logical_and(k > 0, k < last))
    def _():
        for r in range(0, rows, part):
            back_ref[r : r + part, :] += dot_nt(x_ref[r : r + part, :], down_ref[...])

    @pl.when(k == last)
    def _():
        for copy in copies:
            copy.wait()
        for r in range(0, rows, part):
            here = slice(r, r + part)
            score = jnp.zeros((part, LANES), jnp.float32)
            for c in range(0, ffw, part):
                cols = slice(c, c + part)
                back = back_ref[here, cols] + dot_nt(x_ref[here, :], down_ref[cols, :])
                gate = gate_ref[here, cols].astype(jnp.float32)
                up = up_ref[here, cols].astype(jnp.float32)
                sig = 1.0 / (1.0 + jnp.exp(-gate))
                up_grad = back * (gate * sig)
                hidden_ref[here, ffw + c : ffw + c + part] = up_grad.astype(jnp.bfloat16)
                hidden_ref[here, cols] = (back * up * sig * (1.0 + gate * (1.0 - sig))).astype(jnp.bfloat16)
                term = up_grad * up
                for lane in range(0, part, LANES):
                    score = score + term[:, lane : lane + LANES]
            score = jnp.sum(score, axis=1, keepdims=True)
            score_ref[here, :] = jnp.broadcast_to(score, (part, LANES)).astype(jnp.bfloat16)


def hidden_grads(rows_in, down, gate, up, score_at):
    slots, width = rows_in.shape
    ffw = down.shape[0]
    block = 1024
    return pl.pallas_call(
        hidden_kernel,
        grid=(width // block,),
        in_specs=[
            pl.BlockSpec((slots, block), lambda k: (0, k)),
            pl.BlockSpec((ffw, block), lambda k: (0, k)),
            pl.BlockSpec(memory_space=pl.ANY),
            pl.BlockSpec(memory_space=pl.ANY),
        ],
        out_specs=[
            pl.BlockSpec((slots, 2 * ffw), lambda k: (0, 0)),
            pl.BlockSpec((slots, LANES), lambda k: (0, score_at // LANES)),
        ],
        out_shape=[
            jax.ShapeDtypeStruct((slots, 2 * ffw), jnp.bfloat16),
            pltpu.HBM((slots, score_at + LANES), jnp.bfloat16),
        ],
        scratch_shapes=[
            pltpu.VMEM((slots, ffw), jnp.float32),
            pltpu.VMEM((slots, ffw), jnp.bfloat16),
            pltpu.VMEM((slots, ffw), jnp.bfloat16),
            pltpu.SemaphoreType.DMA((2,)),
        ],
        compiler_params=pltpu.CompilerParams(vmem_limit_bytes=44 * MIB),
        cost_estimate=pl.CostEstimate(flops=1, bytes_accessed=1, transcendentals=0),
        name="hidden_grads",
    )(rows_in, *[pltpu.with_memory_space_constraint(a, pltpu.HBM) for a in (down, gate, up)])


def slot_kernel(hidden_ref, gate_w_ref, up_w_ref, *refs):
    out_ref = refs[-1]
    ffw = gate_w_ref.shape[1]
    part = 256
    for r in range(0, out_ref.shape[0], part):
        here = slice(r, r + part)
        out_ref[here, :] = (
            dot_nt(hidden_ref[here, :ffw], gate_w_ref[...]) + dot_nt(hidden_ref[here, ffw:], up_w_ref[...])
        ).astype(jnp.bfloat16)


def slot_grads(hidden, gate_w, up_w, start, width, into=None):
    slots = hidden.shape[0]
    ffw = gate_w.shape[1]
    block = 512
    first = start // block
    before = () if into is None else (into,)
    cost = pl.CostEstimate(flops=1, bytes_accessed=1, transcendentals=0)
    if into is None:
        cost = pl.CostEstimate(
            flops=4 * slots * width * ffw,
            bytes_accessed=2 * (slots * width + 2 * ffw * width + 2 * slots * ffw),
            transcendentals=0,
        )
    return pl.pallas_call(
        slot_kernel,
        grid=(width // block,),
        in_specs=[
            pl.BlockSpec((slots, 2 * ffw), lambda j: (0, 0)),
            pl.BlockSpec((block, ffw), lambda j: (first + j, 0)),
            pl.BlockSpec((block, ffw), lambda j: (first + j, 0)),
        ]
        + [pl.BlockSpec(memory_space=pl.ANY)] * len(before),
        out_specs=pl.BlockSpec((slots, block), lambda j: (0, j)),
        out_shape=pltpu.HBM((slots, width if into is None else into.shape[1]), jnp.bfloat16),
        input_output_aliases={3: 0} if before else {},
        compiler_params=pltpu.CompilerParams(vmem_limit_bytes=32 * MIB),
        cost_estimate=cost,
        name="slot_grads",
    )(
        hidden,
        pltpu.with_memory_space_constraint(gate_w, pltpu.HBM),
        pltpu.with_memory_space_constraint(up_w, pltpu.HBM),
        *before,
    )


def mix_kernel(slot_ref, weight_ref, mix_ref):
    slot = lax.broadcasted_iota(jnp.int32, mix_ref.shape, 1)
    mix = jnp.zeros(mix_ref.shape, jnp.float32)
    for k in range(slot_ref.shape[1]):
        mix = mix + jnp.where(slot_ref[:, k : k + 1] == slot, weight_ref[:, k : k + 1], 0.0)
    mix_ref[...] = mix.astype(jnp.bfloat16)


def mix_weights(slot, weight, slots):
    return pl.pallas_call(
        mix_kernel,
        out_shape=jax.ShapeDtypeStruct((slot.shape[0], slots), jnp.bfloat16),
        name="mix_weights",
    )(slot, weight)


def combine_kernel(mix_ref, rows_ref, *refs):
    refs[-1][...] = jnp.dot(mix_ref[...], rows_ref[...], preferred_element_type=jnp.float32).astype(jnp.bfloat16)


def combine(mix, returned, start, cols, width, earlier=None):
    slots = returned.shape[0]
    tokens = mix.shape[0]
    block = 1024
    first = start // block
    before = () if earlier is None else (earlier,)
    return pl.pallas_call(
        combine_kernel,
        grid=(cols // block,),
        in_specs=[
            pl.BlockSpec(mix.shape, lambda j: (0, 0)),
            pl.BlockSpec((slots, block), lambda j: (0, j)),
        ]
        + [pl.BlockSpec(memory_space=pl.ANY)] * len(before),
        out_specs=pl.BlockSpec((tokens, block), lambda j: (0, first + j)),
        out_shape=jax.ShapeDtypeStruct((tokens, width), jnp.bfloat16),
        input_output_aliases={2: 0} if before else {},
        compiler_params=pltpu.CompilerParams(vmem_limit_bytes=32 * MIB),
        cost_estimate=pl.CostEstimate(
            flops=10**12 if earlier is None else 2 * slots * tokens * cols,
            bytes_accessed=2 * (slots + tokens) * cols,
            transcendentals=0,
        ),
        name="combine",
    )(mix, returned, *before)


def term_kernel(place_ref, *refs):
    packs, (own_ref, *sent_refs), term_ref = refs[:4], refs[4:8], refs[8]
    cols = packs[0].shape[1] // 2
    term = None
    for pack in packs:
        one = lax.dot_general(
            pack[:, :cols], pack[:, cols:], (((0,), (0,)), ((), ())), preferred_element_type=jnp.float32
        )
        term = one if term is None else term + one
    term_ref[...] = term
    rows = cols // 16
    for k, out_ref in enumerate((own_ref, *sent_refs)):
        at = lax.rem(place_ref[0] + k, 4)
        for z in range(4):
            start = pl.multiple_of(z * 4 * rows + at * rows, rows)
            out_ref[z * rows : (z + 1) * rows, :] = term_ref[pl.ds(start, rows), :].astype(out_ref.dtype)


def split_terms(place, packs):
    cols = packs[0].shape[1] // 2
    shape = (cols // 4, cols)
    return pl.pallas_call(
        term_kernel,
        in_specs=[pl.BlockSpec(memory_space=pltpu.SMEM)] + [pl.BlockSpec(memory_space=pltpu.VMEM)] * 4,
        out_specs=[pl.BlockSpec(memory_space=pltpu.VMEM)] * 4,
        out_shape=[jax.ShapeDtypeStruct(shape, jnp.float32)] + [jax.ShapeDtypeStruct(shape, jnp.bfloat16)] * 3,
        scratch_shapes=[pltpu.VMEM((cols, cols), jnp.float32)],
        compiler_params=pltpu.CompilerParams(vmem_limit_bytes=16 * MIB),
        cost_estimate=pl.CostEstimate(flops=1, bytes_accessed=1, transcendentals=0),
        name="split_terms",
    )(place, *packs)


def shift(array, axes, steps):
    sizes = [lax.axis_size(axis) for axis in axes]
    pairs = []
    for source in range(math.prod(sizes)):
        target, rest, scale = 0, source, 1
        for size, step in zip(reversed(sizes), reversed(steps)):
            target += (rest % size + step) % size * scale
            rest, scale = rest // size, scale * size
        pairs.append((source, target))
    return lax.ppermute(array, axes, pairs)


def pick(array, at, dim):
    return lax.dynamic_index_in_dim(array, at, dim, keepdims=False)


def by_core(core, first, second):
    return jnp.where(core == 0, first, second), jnp.where(core == 0, second, first)


def body(
    value_input,
    value_grad,
    value_weight,
    out_grad,
    route_ids,
    route_slots,
    seq_lengths,
    route_weights,
    gate_act,
    up_act,
    w_gate,
    w_up,
    w_down,
):
    tokens, width = out_grad.shape
    feats = value_grad.shape[1]
    devices, capacity, ffw = gate_act.shape[1:]
    slots = devices * capacity
    x_lo, z, core, x_hi, y = (lax.axis_index(axis) for axis in PLACE)
    half, cols = width // 2, width // 16
    in_parts = ((0, 1024), (1024, 3072))

    live = jnp.arange(tokens, dtype=jnp.int32) < seq_lengths[0]
    slot = jnp.where(live[:, None], in_order(route_ids) * capacity + route_slots, -1)

    with jax.named_scope("value_first"):
        beside = shift(value_weight, ("x_lo",), (1,))

    with jax.named_scope("dispatch"):
        send = build_rows(seq_lengths, route_ids.T, route_slots.T, out_grad, slots)
        send, beside, value_in, gate_act, up_act = lax.optimization_barrier(
            (send, beside, value_input, gate_act, up_act)
        )
        routed = exchange(send.reshape(devices, capacity, width), ORDER).reshape(slots, width)

    with jax.named_scope("value_second"):
        pair = jnp.stack(by_core(x_lo, value_weight, beside))
        halves = value_in.reshape(tokens, 8, 2, cols)
        own, other = by_core(core, halves[:, :, 0], halves[:, :, 1])
        other = jnp.concatenate([other.reshape(tokens, half), value_grad], axis=1)
        other = shift(other, ("core",), (1,))
        inputs = jnp.concatenate([own.reshape(tokens, half), other[:, :half]])
        inputs = inputs.reshape(2 * tokens, 2, 4, 2, cols // 2)
        grads = jnp.concatenate([value_grad, other[:, half:]])

        def along_x(a, b):
            at = (0, (x_lo + a) % 2, 0, (x_hi + b) % 2, 0)
            part = lax.dynamic_slice(inputs, at, (2 * tokens, 1, 4, 1, cols // 2))
            return jnp.concatenate([part.reshape(2 * tokens, 2 * cols), grads], axis=1)

        steps = ((0, 1), (1, 0), (1, 1))
        kept = along_x(0, 0)
        packs = [along_x(*step) for step in steps]
        mix = mix_weights(slot, route_weights.astype(jnp.float32), slots)
        gate_act, up_act = (
            a.reshape(*SIZES, capacity, ffw).transpose(1, 4, 3, 2, 0, 5, 6).reshape(slots, ffw)
            for a in (gate_act, up_act)
        )
        below, above = shift(pair, ("z",), (1,)), shift(pair, ("z",), (3,))
        arrived = [shift(pack, ("x_lo", "x_hi"), step) for pack, step in zip(packs, steps)]
        routed, mix, kept, gate_act, up_act, *_ = lax.optimization_barrier(
            (routed, mix, kept, gate_act, up_act, pair, *packs)
        )

    with jax.named_scope("experts"):
        hidden, score = hidden_grads(routed, w_down[0], gate_act, up_act, in_parts[0][1])
        slot_first = slot_grads(hidden, w_gate[0], w_up[0], *in_parts[0], score)
        slot_second = slot_grads(hidden, w_gate[0], w_up[0], *in_parts[1])

    with jax.named_scope("value_third"):
        held = lax.optimization_barrier((slot_first, below, above, *arrived))
        slot_first, below, above = held[:3]
        total, *sent = split_terms(y.reshape(1), (kept, *held[3:]))
        terms = [shift(t, ("y",), (k,)) for t, k in zip(sent, (1, 2, 3))]
        halfway = [shift(below[0], ("z",), (1,)), shift(above[1], ("z",), (3,))]

    with jax.named_scope("return"):
        first = exchange(slot_first.reshape(devices, capacity, -1), ORDER).reshape(slots, -1)
        second = exchange(slot_second.reshape(devices, capacity, -1), ORDER).reshape(slots, -1)
        moe_input_grad = combine(mix, first, *in_parts[0], width)
        moe_input_grad, *held = lax.optimization_barrier((moe_input_grad, *halfway, *terms))
        halfway, terms = held[:2], held[2:]
        scores = first[:, in_parts[0][1]].astype(jnp.float32)
        weight_grad = jnp.sum(
            jnp.where(slot[:, :, None] == jnp.arange(slots, dtype=jnp.int32), scores, 0.0), axis=2
        ).astype(jnp.bfloat16)
        moe_input_grad = combine(mix, second, *in_parts[1], width, moe_input_grad)

    with jax.named_scope("value_last"):
        for part in terms:
            total = total + part.astype(jnp.float32)
        total = total.reshape(4, cols // 8, feats)
        last = [shift(pick(total, (z + k) % 4, 0), ("z",), (k,)) for k in (1, 2, 3)]
        total = pick(total, z, 0)

        ring = jnp.stack([pair, above, jnp.stack(halfway), below])
        across = shift(ring, ("core",), (1,))

        def products(weight):
            out = jnp.einsum("tk,ixrk->ixtr", value_grad, weight, preferred_element_type=jnp.float32)
            out = out.astype(jnp.bfloat16)
            return lax.dynamic_slice_in_dim(jnp.concatenate([out, out]), (4 - z) % 4, 4, axis=0)

        both = jnp.stack(by_core(core, products(ring), products(across)))
        value_input_grad = both.transpose(3, 2, 1, 0, 4).reshape(tokens, width)

    with jax.named_scope("finish"):
        moe_input_grad, total, *last = lax.optimization_barrier((moe_input_grad, total, *last))
        value_weight_grad = total + last[0] + last[1] + last[2]
    return (moe_input_grad, weight_grad, value_input_grad, value_weight_grad)


def solution(mesh):
    places = Mesh(mesh.devices.reshape(SIZES), PLACE)
    split = P(PLACE, None)
    return jax.shard_map(
        body,
        mesh=places,
        in_specs=(
            split,
            split,
            P(PLACE[:3], None),
            split,
            split,
            split,
            P(PLACE),
            split,
            P(PLACE, None, None, None),
            P(PLACE, None, None, None),
            P(PLACE, None, None),
            P(PLACE, None, None),
            P(PLACE, None, None),
        ),
        out_specs=(split, split, split, split),
        check_vma=False,
    )
```

```python
import math

import jax
import jax.numpy as jnp
from jax import lax
from jax.experimental import pallas as pl
from jax.experimental.pallas import tpu as pltpu
from jax.sharding import Mesh, PartitionSpec as P

PLACE = ("x_lo", "z", "core", "x_hi", "y")
SIZES = (2, 4, 2, 2, 4)
ORDER = ("z", "y", "x_lo", "x_hi", "core")
MIB = 1024 * 1024
LANES = 128
CAPACITY = 8
NT = (((1,), (1,)), ((), ()))


def dot_nt(left, right):
    return lax.dot_general(left, right, NT, preferred_element_type=jnp.float32)


def in_order(device):
    x_lo, z, core, x_hi, y = device // 64, device // 16 % 4, device // 8 % 2, device // 4 % 2, device % 4
    return (((z * 4 + y) * 2 + x_lo) * 2 + x_hi) * 2 + core


def exchange(array, axes):
    return lax.all_to_all(array, axes, split_axis=0, concat_axis=0, tiled=True)


def rows_kernel(length_ref, ids_ref, slots_ref, grad_ref, out_ref):
    rows, width = out_ref.shape
    top, tokens = ids_ref.shape
    live = lax.broadcasted_iota(jnp.int32, (1, tokens), 1) < length_ref[0]
    slot = lax.broadcasted_iota(jnp.int32, (rows, tokens), 0) + pl.program_id(0) * rows
    hit = None
    for k in range(top):
        name = in_order(ids_ref[k : k + 1, :]) * CAPACITY + slots_ref[k : k + 1, :]
        name = jnp.where(live, name, -1)
        hit = name == slot if hit is None else hit | (name == slot)
    pick = jnp.where(hit, 1.0, 0.0).astype(jnp.bfloat16)
    step = 1024
    for c in range(0, width, step):
        out_ref[:, c : c + step] = jnp.dot(
            pick, grad_ref[:, c : c + step], preferred_element_type=jnp.float32
        ).astype(jnp.bfloat16)


def build_rows(seq_lengths, ids_t, slots_t, out_grad, slots):
    tokens, width = out_grad.shape
    rows = 256
    return pl.pallas_call(
        rows_kernel,
        grid=(slots // rows,),
        in_specs=[
            pl.BlockSpec(memory_space=pltpu.SMEM),
            pl.BlockSpec(ids_t.shape, lambda i: (0, 0)),
            pl.BlockSpec(slots_t.shape, lambda i: (0, 0)),
            pl.BlockSpec((tokens, width), lambda i: (0, 0)),
        ],
        out_specs=pl.BlockSpec((rows, width), lambda i: (i, 0)),
        out_shape=pltpu.HBM((slots, width), jnp.bfloat16),
        compiler_params=pltpu.CompilerParams(vmem_limit_bytes=32 * MIB),
        cost_estimate=pl.CostEstimate(
            flops=2 * slots * tokens * width, bytes_accessed=2 * (slots + tokens) * width, transcendentals=0
        ),
        name="build_rows",
    )(seq_lengths, *[pltpu.with_memory_space_constraint(a, pltpu.HBM) for a in (ids_t, slots_t, out_grad)])


def hidden_kernel(x_ref, down_ref, gate_hbm, up_hbm, hidden_ref, score_ref, back_ref, gate_ref, up_ref, sems):
    k = pl.program_id(0)
    last = pl.num_programs(0) - 1
    rows, ffw = back_ref.shape
    part = 256
    copies = [
        pltpu.make_async_copy(gate_hbm, gate_ref, sems.at[0]),
        pltpu.make_async_copy(up_hbm, up_ref, sems.at[1]),
    ]

    @pl.when(k == 0)
    def _():
        for copy in copies:
            copy.start()
        for r in range(0, rows, part):
            back_ref[r : r + part, :] = dot_nt(x_ref[r : r + part, :], down_ref[...])

    @pl.when(jnp.logical_and(k > 0, k < last))
    def _():
        for r in range(0, rows, part):
            back_ref[r : r + part, :] += dot_nt(x_ref[r : r + part, :], down_ref[...])

    @pl.when(k == last)
    def _():
        for copy in copies:
            copy.wait()
        for r in range(0, rows, part):
            here = slice(r, r + part)
            score = jnp.zeros((part, LANES), jnp.float32)
            for c in range(0, ffw, part):
                cols = slice(c, c + part)
                back = back_ref[here, cols] + dot_nt(x_ref[here, :], down_ref[cols, :])
                gate = gate_ref[here, cols].astype(jnp.float32)
                up = up_ref[here, cols].astype(jnp.float32)
                sig = 1.0 / (1.0 + jnp.exp(-gate))
                up_grad = back * (gate * sig)
                hidden_ref[here, ffw + c : ffw + c + part] = up_grad.astype(jnp.bfloat16)
                hidden_ref[here, cols] = (back * up * sig * (1.0 + gate * (1.0 - sig))).astype(jnp.bfloat16)
                term = up_grad * up
                for lane in range(0, part, LANES):
                    score = score + term[:, lane : lane + LANES]
            score = jnp.sum(score, axis=1, keepdims=True)
            score_ref[here, :] = jnp.broadcast_to(score, (part, LANES)).astype(jnp.bfloat16)


def hidden_grads(rows_in, down, gate, up, score_at):
    slots, width = rows_in.shape
    ffw = down.shape[0]
    block = 1024
    return pl.pallas_call(
        hidden_kernel,
        grid=(width // block,),
        in_specs=[
            pl.BlockSpec((slots, block), lambda k: (0, k)),
            pl.BlockSpec((ffw, block), lambda k: (0, k)),
            pl.BlockSpec(memory_space=pl.ANY),
            pl.BlockSpec(memory_space=pl.ANY),
        ],
        out_specs=[
            pl.BlockSpec((slots, 2 * ffw), lambda k: (0, 0)),
            pl.BlockSpec((slots, LANES), lambda k: (0, score_at // LANES)),
        ],
        out_shape=[
            jax.ShapeDtypeStruct((slots, 2 * ffw), jnp.bfloat16),
            pltpu.HBM((slots, score_at + LANES), jnp.bfloat16),
        ],
        scratch_shapes=[
            pltpu.VMEM((slots, ffw), jnp.float32),
            pltpu.VMEM((slots, ffw), jnp.bfloat16),
            pltpu.VMEM((slots, ffw), jnp.bfloat16),
            pltpu.SemaphoreType.DMA((2,)),
        ],
        compiler_params=pltpu.CompilerParams(vmem_limit_bytes=44 * MIB),
        cost_estimate=pl.CostEstimate(flops=1, bytes_accessed=1, transcendentals=0),
        name="hidden_grads",
    )(rows_in, *[pltpu.with_memory_space_constraint(a, pltpu.HBM) for a in (down, gate, up)])


def slot_kernel(hidden_ref, gate_w_ref, up_w_ref, *refs):
    out_ref = refs[-1]
    ffw = gate_w_ref.shape[1]
    part = 256
    for r in range(0, out_ref.shape[0], part):
        here = slice(r, r + part)
        out_ref[here, :] = (
            dot_nt(hidden_ref[here, :ffw], gate_w_ref[...]) + dot_nt(hidden_ref[here, ffw:], up_w_ref[...])
        ).astype(jnp.bfloat16)


def slot_grads(hidden, gate_w, up_w, start, width, into=None):
    slots = hidden.shape[0]
    ffw = gate_w.shape[1]
    block = 512
    first = start // block
    before = () if into is None else (into,)
    cost = pl.CostEstimate(flops=1, bytes_accessed=1, transcendentals=0)
    if into is None:
        cost = pl.CostEstimate(
            flops=4 * slots * width * ffw,
            bytes_accessed=2 * (slots * width + 2 * ffw * width + 2 * slots * ffw),
            transcendentals=0,
        )
    return pl.pallas_call(
        slot_kernel,
        grid=(width // block,),
        in_specs=[
            pl.BlockSpec((slots, 2 * ffw), lambda j: (0, 0)),
            pl.BlockSpec((block, ffw), lambda j: (first + j, 0)),
            pl.BlockSpec((block, ffw), lambda j: (first + j, 0)),
        ]
        + [pl.BlockSpec(memory_space=pl.ANY)] * len(before),
        out_specs=pl.BlockSpec((slots, block), lambda j: (0, j)),
        out_shape=pltpu.HBM((slots, width if into is None else into.shape[1]), jnp.bfloat16),
        input_output_aliases={3: 0} if before else {},
        compiler_params=pltpu.CompilerParams(vmem_limit_bytes=32 * MIB),
        cost_estimate=cost,
        name="slot_grads",
    )(
        hidden,
        pltpu.with_memory_space_constraint(gate_w, pltpu.HBM),
        pltpu.with_memory_space_constraint(up_w, pltpu.HBM),
        *before,
    )


def mix_kernel(slot_ref, weight_ref, mix_ref):
    slot = lax.broadcasted_iota(jnp.int32, mix_ref.shape, 1)
    mix = jnp.zeros(mix_ref.shape, jnp.float32)
    for k in range(slot_ref.shape[1]):
        mix = mix + jnp.where(slot_ref[:, k : k + 1] == slot, weight_ref[:, k : k + 1], 0.0)
    mix_ref[...] = mix.astype(jnp.bfloat16)


def mix_weights(slot, weight, slots):
    return pl.pallas_call(
        mix_kernel,
        out_shape=jax.ShapeDtypeStruct((slot.shape[0], slots), jnp.bfloat16),
        name="mix_weights",
    )(slot, weight)


def combine_kernel(mix_ref, rows_ref, *refs):
    refs[-1][...] = jnp.dot(mix_ref[...], rows_ref[...], preferred_element_type=jnp.float32).astype(jnp.bfloat16)


def combine(mix, returned, start, cols, width, earlier=None):
    slots = returned.shape[0]
    tokens = mix.shape[0]
    block = 1024
    first = start // block
    before = () if earlier is None else (earlier,)
    return pl.pallas_call(
        combine_kernel,
        grid=(cols // block,),
        in_specs=[
            pl.BlockSpec(mix.shape, lambda j: (0, 0)),
            pl.BlockSpec((slots, block), lambda j: (0, j)),
        ]
        + [pl.BlockSpec(memory_space=pl.ANY)] * len(before),
        out_specs=pl.BlockSpec((tokens, block), lambda j: (0, first + j)),
        out_shape=jax.ShapeDtypeStruct((tokens, width), jnp.bfloat16),
        input_output_aliases={2: 0} if before else {},
        compiler_params=pltpu.CompilerParams(vmem_limit_bytes=32 * MIB),
        cost_estimate=pl.CostEstimate(
            flops=10**12 if earlier is None else 2 * slots * tokens * cols,
            bytes_accessed=2 * (slots + tokens) * cols,
            transcendentals=0,
        ),
        name="combine",
    )(mix, returned, *before)


def term_kernel(place_ref, *refs):
    packs, (own_ref, *sent_refs), term_ref = refs[:4], refs[4:8], refs[8]
    cols = packs[0].shape[1] // 2
    term = None
    for pack in packs:
        one = lax.dot_general(
            pack[:, :cols], pack[:, cols:], (((0,), (0,)), ((), ())), preferred_element_type=jnp.float32
        )
        term = one if term is None else term + one
    term_ref[...] = term
    rows = cols // 16
    for k, out_ref in enumerate((own_ref, *sent_refs)):
        at = lax.rem(place_ref[0] + k, 4)
        for z in range(4):
            start = pl.multiple_of(z * 4 * rows + at * rows, rows)
            out_ref[z * rows : (z + 1) * rows, :] = term_ref[pl.ds(start, rows), :].astype(out_ref.dtype)


def split_terms(place, packs):
    cols = packs[0].shape[1] // 2
    shape = (cols // 4, cols)
    return pl.pallas_call(
        term_kernel,
        in_specs=[pl.BlockSpec(memory_space=pltpu.SMEM)] + [pl.BlockSpec(memory_space=pltpu.VMEM)] * 4,
        out_specs=[pl.BlockSpec(memory_space=pltpu.VMEM)] * 4,
        out_shape=[jax.ShapeDtypeStruct(shape, jnp.float32)] + [jax.ShapeDtypeStruct(shape, jnp.bfloat16)] * 3,
        scratch_shapes=[pltpu.VMEM((cols, cols), jnp.float32)],
        compiler_params=pltpu.CompilerParams(vmem_limit_bytes=16 * MIB),
        cost_estimate=pl.CostEstimate(flops=1, bytes_accessed=1, transcendentals=0),
        name="split_terms",
    )(place, *packs)


def shift(array, axes, steps):
    sizes = [lax.axis_size(axis) for axis in axes]
    pairs = []
    for source in range(math.prod(sizes)):
        target, rest, scale = 0, source, 1
        for size, step in zip(reversed(sizes), reversed(steps)):
            target += (rest % size + step) % size * scale
            rest, scale = rest // size, scale * size
        pairs.append((source, target))
    return lax.ppermute(array, axes, pairs)


def pick(array, at, dim):
    return lax.dynamic_index_in_dim(array, at, dim, keepdims=False)


def by_core(core, first, second):
    return jnp.where(core == 0, first, second), jnp.where(core == 0, second, first)


def body(
    value_input,
    value_grad,
    value_weight,
    out_grad,
    route_ids,
    route_slots,
    seq_lengths,
    route_weights,
    gate_act,
    up_act,
    w_gate,
    w_up,
    w_down,
):
    tokens, width = out_grad.shape
    feats = value_grad.shape[1]
    devices, capacity, ffw = gate_act.shape[1:]
    slots = devices * capacity
    x_lo, z, core, x_hi, y = (lax.axis_index(axis) for axis in PLACE)
    half, cols = width // 2, width // 16
    in_parts = ((0, 1024), (1024, 3072))

    live = jnp.arange(tokens, dtype=jnp.int32) < seq_lengths[0]
    slot = jnp.where(live[:, None], in_order(route_ids) * capacity + route_slots, -1)

    with jax.named_scope("value_first"):
        beside = shift(value_weight, ("x_lo",), (1,))

    with jax.named_scope("dispatch"):
        send = build_rows(seq_lengths, route_ids.T, route_slots.T, out_grad, slots)
        send, beside, value_in, gate_act, up_act = lax.optimization_barrier(
            (send, beside, value_input, gate_act, up_act)
        )
        routed = exchange(send.reshape(devices, capacity, width), ORDER).reshape(slots, width)

    with jax.named_scope("value_second"):
        pair = jnp.stack(by_core(x_lo, value_weight, beside))
        halves = value_in.reshape(tokens, 8, 2, cols)
        own, other = by_core(core, halves[:, :, 0], halves[:, :, 1])
        other = jnp.concatenate([other.reshape(tokens, half), value_grad], axis=1)
        other = shift(other, ("core",), (1,))
        inputs = jnp.concatenate([own.reshape(tokens, half), other[:, :half]])
        inputs = inputs.reshape(2 * tokens, 2, 4, 2, cols // 2)
        grads = jnp.concatenate([value_grad, other[:, half:]])

        def along_x(a, b):
            at = (0, (x_lo + a) % 2, 0, (x_hi + b) % 2, 0)
            part = lax.dynamic_slice(inputs, at, (2 * tokens, 1, 4, 1, cols // 2))
            return jnp.concatenate([part.reshape(2 * tokens, 2 * cols), grads], axis=1)

        steps = ((0, 1), (1, 0), (1, 1))
        kept = along_x(0, 0)
        packs = [along_x(*step) for step in steps]
        mix = mix_weights(slot, route_weights.astype(jnp.float32), slots)
        gate_act, up_act = (
            a.reshape(*SIZES, capacity, ffw).transpose(1, 4, 0, 3, 2, 5, 6).reshape(slots, ffw)
            for a in (gate_act, up_act)
        )
        below, above = shift(pair, ("z",), (1,)), shift(pair, ("z",), (3,))
        arrived = [shift(pack, ("x_lo", "x_hi"), step) for pack, step in zip(packs, steps)]
        routed, mix, kept, gate_act, up_act, *_ = lax.optimization_barrier(
            (routed, mix, kept, gate_act, up_act, pair, *packs)
        )

    with jax.named_scope("experts"):
        hidden, score = hidden_grads(routed, w_down[0], gate_act, up_act, in_parts[0][1])
        slot_first = slot_grads(hidden, w_gate[0], w_up[0], *in_parts[0], score)
        slot_second = slot_grads(hidden, w_gate[0], w_up[0], *in_parts[1])

    with jax.named_scope("value_third"):
        held = lax.optimization_barrier((slot_first, below, above, *arrived))
        slot_first, below, above = held[:3]
        total, *sent = split_terms(y.reshape(1), (kept, *held[3:]))
        terms = [shift(t, ("y",), (k,)) for t, k in zip(sent, (1, 2, 3))]
        halfway = [shift(below[0], ("z",), (1,)), shift(above[1], ("z",), (3,))]

    with jax.named_scope("return"):
        first = exchange(slot_first.reshape(devices, capacity, -1), ORDER).reshape(slots, -1)
        second = exchange(slot_second.reshape(devices, capacity, -1), ORDER).reshape(slots, -1)
        moe_input_grad = combine(mix, first, *in_parts[0], width)
        moe_input_grad, *held = lax.optimization_barrier((moe_input_grad, *halfway, *terms))
        halfway, terms = held[:2], held[2:]
        scores = first[:, in_parts[0][1]].astype(jnp.float32)
        weight_grad = jnp.sum(
            jnp.where(slot[:, :, None] == jnp.arange(slots, dtype=jnp.int32), scores, 0.0), axis=2
        ).astype(jnp.bfloat16)
        moe_input_grad = combine(mix, second, *in_parts[1], width, moe_input_grad)

    with jax.named_scope("value_last"):
        for part in terms:
            total = total + part.astype(jnp.float32)
        total = total.reshape(4, cols // 8, feats)
        last = [shift(pick(total, (z + k) % 4, 0), ("z",), (k,)) for k in (1, 2, 3)]
        total = pick(total, z, 0)

        ring = jnp.stack([pair, above, jnp.stack(halfway), below])
        across = shift(ring, ("core",), (1,))

        def products(weight):
            out = jnp.einsum("tk,ixrk->ixtr", value_grad, weight, preferred_element_type=jnp.float32)
            out = out.astype(jnp.bfloat16)
            return lax.dynamic_slice_in_dim(jnp.concatenate([out, out]), (4 - z) % 4, 4, axis=0)

        both = jnp.stack(by_core(core, products(ring), products(across)))
        value_input_grad = both.transpose(3, 2, 1, 0, 4).reshape(tokens, width)

    with jax.named_scope("finish"):
        moe_input_grad, total, *last = lax.optimization_barrier((moe_input_grad, total, *last))
        value_weight_grad = total + last[0] + last[1] + last[2]
    return (moe_input_grad, weight_grad, value_input_grad, value_weight_grad)


def solution(mesh):
    places = Mesh(mesh.devices.reshape(SIZES), PLACE)
    split = P(PLACE, None)
    return jax.shard_map(
        body,
        mesh=places,
        in_specs=(
            split,
            split,
            P(PLACE[:3], None),
            split,
            split,
            split,
            P(PLACE),
            split,
            P(PLACE, None, None, None),
            P(PLACE, None, None, None),
            P(PLACE, None, None),
            P(PLACE, None, None),
            P(PLACE, None, None),
        ),
        out_specs=(split, split, split, split),
        check_vma=False,
    )
```
